32 devices in a mesh: grp: 2 (over core), gz: 8 (over z, y), xy: 2 (over x).
Axes of the slice: x: 2, y: 2, z: 4, core: 2. Of those that a mesh axis runs over, the one named last changes fastest.
Arguments:
- velocity: float32 [2, 3, 8, 512, 512], P('grp', None, 'gz', 'xy'), may hold values from -6 to 6
- fringe_columns: int32 [128], replicated, may hold values from 0 to 511, as said below
Outputs:
- velocity_next: float32 [2, 3, 8, 512, 512], P('grp', None, 'gz', 'xy')
The draws below stay inside these ranges and needn't reach their ends.
Inputs may be any that keep to these rules, and one draw needn't show every extreme that they name: `fringe_columns`: 128 consecutive precursor columns, counted modulo 512, from a start that varies; the run always passes column 511 and wraps to column 0.
All inputs are finite; a program needn't handle non-finite values.
Results may differ from the reference program's by a relative error of at most 0.0001.
Values sent between devices are 32-bit elements; how exact they have to be, the bound alone decides.
A program may use at most 64 MiB of HBM per device.

```python
import math
import jax
import jax.numpy as jnp
from jax import lax

NX = 512
NY = 512
STEPS = 2
NZ = 8
FRINGE = 128


def draw_fringe_columns(key, part):
    start_key = jax.random.fold_in(key, 7919)
    first = jax.random.randint(start_key, (), NX - FRINGE + 1, NX, dtype=jnp.int32)
    return ((first + jnp.arange(FRINGE, dtype=jnp.int32)) % NX).astype(jnp.int32)


def block_scale(own_key, dims, pieces, least, high):
    def one(axis_at, parts):
        steps = jax.random.uniform(jax.random.fold_in(jax.random.fold_in(own_key, 6), axis_at), (parts,), jnp.float32, least / len(pieces), high / len(pieces))
        return jnp.repeat(jnp.exp(steps), dims[axis_at] // parts).reshape((-1,) + (1,) * (len(dims) - axis_at - 1))

    gain = one(*pieces[0])
    for cut in pieces[1:]:
        gain = gain * one(*cut)
    return gain


def centred(own_key, dims, spread, bound, shards=(), kind=jnp.bfloat16):
    level = block_scale(own_key, dims, shards, -0.22, 0.18) if shards else 1.0
    entries = jax.random.normal(own_key, dims, jnp.float32) * spread * level
    return jnp.minimum(jnp.maximum(entries, -bound), bound).astype(kind)


def setup_inputs(seed: int = 0) -> dict:
    key_of = jax.random.split(jax.random.key(seed), 3)
    velocity = centred(key_of[0], (2, 3, NZ, NY, NX), 1.0, 6.0, ((0, 2), (2, 8), (3, 2)), jnp.float32)
    fringe_columns = draw_fringe_columns(jax.random.fold_in(key_of[2], 71), 0)
    return {"velocity": velocity, "fringe_columns": fringe_columns}


time_step = 0.001
level_gap = 0.05
smag_coeff = 0.16

def spectral_derivative(field, axis):
    moved = jnp.moveaxis(field, axis, -1)
    points = moved.shape[-1]
    wavenumber = jnp.arange(points // 2 + 1)
    wavenumber = jnp.where(wavenumber == points // 2, 0, wavenumber).astype(field.dtype)
    spectrum = jnp.fft.rfft(moved, axis=-1)
    result = jnp.fft.irfft(spectrum * (1j * wavenumber), n=points, axis=-1).astype(field.dtype)
    return jnp.moveaxis(result, -1, axis)

def vertical_derivative(field):
    padded = jnp.pad(field, ((0, 0), (1, 1), (0, 0), (0, 0)))
    return (padded[:, 2:] - padded[:, :-2]) / (2.0 * level_gap)

def tendency(velocity_now):
    along_x = spectral_derivative(velocity_now, 3)
    along_y = spectral_derivative(velocity_now, 2)
    along_z = vertical_derivative(velocity_now)
    gradient = jnp.stack([along_x, along_y, along_z], axis=1)
    strain = 0.5 * (gradient + jnp.swapaxes(gradient, 0, 1))
    delta = (2.0 * math.pi / NX * (2.0 * math.pi / NY) * level_gap) ** (1.0 / 3.0)
    eddy_visc = (smag_coeff * delta) ** 2 * jnp.sqrt(2.0 * lax.optimization_barrier(jnp.sum(strain * strain, axis=(0, 1))))
    stress = 2.0 * eddy_visc[None, None] * strain
    advection = lax.optimization_barrier(jnp.sum(gradient * velocity_now[None], axis=1))
    divergence = spectral_derivative(stress[:, 0], 3) + spectral_derivative(stress[:, 1], 2) + vertical_derivative(stress[:, 2])
    return divergence - advection

def reference(velocity, fringe_columns):
    farm_state = velocity[0]
    precursor = velocity[1]
    offsets = jnp.arange(FRINGE).astype(jnp.float32)
    weights = 0.5 * (1.0 + jnp.cos(jnp.pi * offsets / FRINGE))
    for step_index in range(STEPS):
        farm_state = farm_state + time_step * tendency(farm_state)
        precursor = precursor + time_step * tendency(precursor)
        picked = jnp.take(precursor, fringe_columns, axis=3)
        blended = (1.0 - weights) * farm_state[..., :FRINGE] + weights * picked
        farm_state = jnp.concatenate([blended, farm_state[..., FRINGE:]], axis=3)
    return jnp.stack([farm_state, precursor])
```

```python
import functools
import math

import jax
import jax.numpy as jnp
import ml_dtypes
import numpy as np
from jax import lax
from jax.experimental import pallas as pl
from jax.experimental.pallas import tpu as pltpu
from jax.sharding import PartitionSpec as P

STEPS = 2
CHUNKS = 4
ROWS = 8

time_step = 0.001
level_gap = 0.05
smag_coeff = 0.16
MESH = pl.DeviceIdType.MESH


def derivative_matrix(points):
    offsets = np.arange(points)
    distance = offsets[:, None] - offsets[None, :]
    safe = np.where(distance == 0, 1, distance)
    entries = 0.5 * (1.0 - 2.0 * (distance % 2)) / np.tan(np.pi * safe / points)
    return np.where(distance == 0, 0.0, entries)


def two_parts(matrix):
    single = matrix.astype(np.float32)
    high = single.astype(ml_dtypes.bfloat16)
    low = (single - high.astype(np.float32)).astype(ml_dtypes.bfloat16)
    return np.stack([high, low])


def factored(block):
    rest = block.copy()
    limit = np.abs(block).max() * 2.0**-30
    columns, rows = [], []
    while len(rows) < block.shape[1]:
        row, column = np.unravel_index(np.argmax(np.abs(rest)), rest.shape)
        if abs(rest[row, column]) < limit and len(rows) % 16 == 0:
            break
        if rest[row, column] == 0.0:
            columns.append(np.zeros_like(rest[:, 0]))
            rows.append(np.zeros_like(rest[0]))
            continue
        columns.append(rest[:, column] / rest[row, column])
        rows.append(rest[row].copy())
        rest = rest - np.outer(columns[-1], rows[-1])
    return np.stack(columns, axis=1), np.stack(rows, axis=0)


def halves(value):
    high = value.astype(jnp.bfloat16)
    return high, (value - high.astype(jnp.float32)).astype(jnp.bfloat16)


def dot(left, right):
    return jnp.dot(left, right, preferred_element_type=jnp.float32)


def dot_parts(left, right):
    return dot(left[0], right[0]) + (dot(left[0], right[1]) + dot(left[1], right[0]))


def kernel(
    sizes, in_ref, cols_ref, weight_ref, mx_ref, my_ref, gather_ref, spread_ref, out_ref,
    vel, ret, fin, vhalo, shalo, gx, gy, tend, sx, sy, sz, gsend, grecv, psend, precv,
    send_sem, recv_sem,
):
    n_gz, n_xy, width, scale = sizes
    _, rows_all, cols_all = in_ref.shape
    half = cols_all // 2
    chunk = rows_all // CHUNKS
    grp, gz, xy = lax.axis_index("grp"), lax.axis_index("gz"), lax.axis_index("xy")
    domain = lax.rem(gz, 2)
    pair = gz - domain
    level = pair + grp
    levels = n_gz
    swapped = domain != grp
    has_up = level < levels - 1
    has_down = level > 0
    is_farm = domain == 0

    def at_level(other):
        other = lax.rem(other + levels, levels)
        parity = lax.rem(other, 2)
        return (parity, other - parity + domain, xy)

    up, down = at_level(level + 1), at_level(level - 1)
    swap_to = (domain, pair + grp, xy)
    mid_to = (grp, pair + 1 - domain, xy)
    end_to = (1 - grp, gz, xy)

    def xy_to(offset):
        return (grp, gz, lax.rem(xy + offset, n_xy))

    slots = {}

    def copy(name, source, target, device):
        slot = slots.setdefault(name, len(slots))
        return pltpu.make_async_remote_copy(
            src_ref=source, dst_ref=target, send_sem=send_sem.at[slot],
            recv_sem=recv_sem.at[slot], device_id=device, device_id_type=MESH,
        )

    pending = []

    def start(condition, item):
        pending.append((condition, item))
        if condition is None:
            item.start()
        else:
            pl.when(condition)(item.start)

    def part(ref, k):
        return ref.at[:, pl.ds(k * chunk, chunk), :]

    barrier = pltpu.get_barrier_semaphore()
    for device in [up, down, mid_to, end_to] + [xy_to(o) for o in range(1, n_xy)]:
        pl.semaphore_signal(barrier, inc=1, device_id=device, device_id_type=MESH)

    @pl.when(swapped)
    def _():
        pl.semaphore_signal(barrier, inc=1, device_id=swap_to, device_id_type=MESH)
        pl.semaphore_wait(barrier, 4 + n_xy)

    @pl.when(jnp.logical_not(swapped))
    def _():
        pl.semaphore_wait(barrier, 3 + n_xy)

    def z_copies(kind, s, k):
        source, halo = (vel, vhalo) if kind == "v" else (sz, shalo)
        return (
            copy((kind, s, 0, k), part(source.at[s], k), part(halo.at[s, 0], k), up),
            copy((kind, s, 1, k), part(source.at[s], k), part(halo.at[s, 1], k), down),
        )

    def z_start(kind, s, k):
        upward, downward = z_copies(kind, s, k)
        start(has_up, upward)
        start(has_down, downward)

    def z_wait(kind, s, k):
        upward, downward = z_copies(kind, s, k)
        pl.when(has_down)(upward.wait_recv)
        pl.when(has_up)(downward.wait_recv)

    swap_in = [copy(("in", k), part(in_ref, k), part(vel.at[0], k), swap_to) for k in range(CHUNKS)]
    for k in range(CHUNKS):
        start(swapped, swap_in[k])

    @pl.when(jnp.logical_not(swapped))
    def _():
        vel[0] = in_ref[...]

    @pl.when(level == 0)
    def _():
        for s in range(STEPS):
            vhalo[s, 0] = jnp.zeros_like(vel[0])
            shalo[s, 0] = jnp.zeros_like(vel[0])

    @pl.when(level == levels - 1)
    def _():
        for s in range(STEPS):
            vhalo[s, 1] = jnp.zeros_like(vel[0])
            shalo[s, 1] = jnp.zeros_like(vel[0])

    for k in range(CHUNKS):
        pl.when(swapped)(swap_in[k].wait_recv)
        z_start("v", 0, k)

    picker = jnp.where(
        lax.broadcasted_iota(jnp.int32, (cols_all, width), 0) == cols_ref[...], 1.0, 0.0
    ).astype(jnp.bfloat16)

    def picked(field):
        high = field.astype(jnp.bfloat16)
        rest = field - high.astype(jnp.float32)
        middle = rest.astype(jnp.bfloat16)
        low = (rest - middle.astype(jnp.float32)).astype(jnp.bfloat16)
        return (dot(high, picker) + (dot(middle, picker) + dot(low, picker))) * weight_ref[...]

    def x_derived(field):
        left, right = field[:, :half], field[:, half:]
        total = dot_parts(halves(left + right), (mx_ref[0], mx_ref[1]))
        difference = dot_parts(halves(left - right), (mx_ref[2], mx_ref[3]))
        return jnp.concatenate([total + difference, total - difference], axis=1)

    def compress(index, read):
        def body(c, carry):
            gsend[index, c] = dot_parts((gather_ref[0], gather_ref[1]), halves(read(c)))
            return carry

        lax.fori_loop(0, 3, body, 0)
        for o in range(1, n_xy):
            start(None, compressed(index, o))

    def compressed(index, o):
        return copy(("g", index, o), gsend.at[index], grecv.at[index, o - 1], xy_to(o))

    def received(index, c):
        result = None
        for o in range(1, n_xy):
            term = dot_parts((spread_ref[0, o - 1], spread_ref[1, o - 1]), halves(grecv[index, o - 1, c]))
            result = term if result is None else result + term
        return result

    def g_wait(index):
        for o in range(1, n_xy):
            compressed(index, o).wait_recv()

    z_scale = 1.0 / (2.0 * level_gap)

    for s in range(STEPS):
        compress(2 * s, lambda c: vel[s, c])

        def first(c, carry):
            field = vel[s, c]
            gx[c] = x_derived(field)
            gy[c] = dot_parts((my_ref[0], my_ref[1]), halves(field))
            return carry

        lax.fori_loop(0, 3, first, 0)
        g_wait(2 * s)

        def second(c, carry):
            gy[c] = gy[c] + received(2 * s, c)
            return carry

        if n_xy > 1:
            lax.fori_loop(0, 3, second, 0)

        def pointwise(i, carry):
            rows = pl.ds(pl.multiple_of(i * ROWS, ROWS), ROWS)
            u = [vel[s, c, rows, :] for c in range(3)]
            dx = [gx[c, rows, :] for c in range(3)]
            dy = [gy[c, rows, :] for c in range(3)]
            dz = [(vhalo[s, 1, c, rows, :] - vhalo[s, 0, c, rows, :]) * z_scale for c in range(3)]
            for c in range(3):
                tend[c, rows, :] = -(u[0] * dx[c] + u[1] * dy[c] + u[2] * dz[c])
            xx, yy, zz = dx[0], dy[1], dz[2]
            xy_, xz, yz = 0.5 * (dy[0] + dx[1]), 0.5 * (dz[0] + dx[2]), 0.5 * (dz[1] + dy[2])
            total = xx * xx + yy * yy + zz * zz + 2.0 * (xy_ * xy_ + xz * xz + yz * yz)
            eddy = (2.0 * scale) * jnp.sqrt(2.0 * total)
            xy_, xz, yz = eddy * xy_, eddy * xz, eddy * yz
            sx[0, rows, :] = eddy * xx
            sx[1, rows, :] = xy_
            sx[2, rows, :] = xz
            sy[0, rows, :] = xy_
            sy[1, rows, :] = eddy * yy
            sy[2, rows, :] = yz
            sz[s, 0, rows, :] = xz
            sz[s, 1, rows, :] = yz
            sz[s, 2, rows, :] = eddy * zz
            return carry

        for k in range(CHUNKS):
            z_wait("v", s, k)
            lax.fori_loop(k * chunk // ROWS, (k + 1) * chunk // ROWS, pointwise, 0)
            z_start("s", s, k)

        compress(2 * s + 1, lambda c: sy[c])

        def third(c, carry):
            local = dot_parts((my_ref[0], my_ref[1]), halves(sy[c]))
            tend[c] = tend[c] + x_derived(sx[c]) + local
            return carry

        lax.fori_loop(0, 3, third, 0)
        g_wait(2 * s + 1)

        def fourth(c, carry):
            tend[c] = tend[c] + received(2 * s + 1, c)
            return carry

        if n_xy > 1:
            lax.fori_loop(0, 3, fourth, 0)

        last = s == STEPS - 1

        def updated(k, target):
            def body(i, carry):
                rows = pl.ds(pl.multiple_of(i * ROWS, ROWS), ROWS)
                for c in range(3):
                    along_z = (shalo[s, 1, c, rows, :] - shalo[s, 0, c, rows, :]) * z_scale
                    target[c, rows, :] = vel[s, c, rows, :] + time_step * (tend[c, rows, :] + along_z)
                return carry

            lax.fori_loop(k * chunk // ROWS, (k + 1) * chunk // ROWS, body, 0)

        def pick(k, source):
            rows = pl.ds(k * chunk, chunk)
            for c in range(3):
                psend[s, c, rows, :] = picked(source[c, rows, :])

        def blend(k, source, target):
            rows = pl.ds(k * chunk, chunk)
            for c in range(3):
                own = source[c, rows, :width] * (1.0 - weight_ref[...])
                target[c, rows, :width] = own + precv[s, c, rows, :]

        def fringe_copy(k, device):
            return copy(("f", s, k), part(psend.at[s], k), part(precv.at[s], k), device)

        if not last:
            following = vel.at[s + 1]
            for k in range(CHUNKS):
                z_wait("s", s, k)
                updated(k, following)

                @pl.when(jnp.logical_not(is_farm))
                def _():
                    pick(k, following)

                start(jnp.logical_not(is_farm), fringe_copy(k, mid_to))

                @pl.when(is_farm)
                def _():
                    fringe_copy(k, mid_to).wait_recv()
                    blend(k, following, following)

                z_start("v", s + 1, k)
        else:
            back = [copy(("out", k), part(ret, k), part(fin, k), swap_to) for k in range(CHUNKS)]
            for k in range(CHUNKS):
                z_wait("s", s, k)

                @pl.when(swapped)
                def _():
                    updated(k, ret)

                @pl.when(jnp.logical_not(swapped))
                def _():
                    updated(k, fin)

                start(swapped, back[k])
            for k in range(CHUNKS):
                pl.when(swapped)(back[k].wait_recv)

                @pl.when(grp == 1)
                def _():
                    pick(k, fin)

                start(grp == 1, fringe_copy(k, end_to))
                rows = pl.ds(k * chunk, chunk)
                out_ref[:, rows, :] = fin[:, rows, :]

                @pl.when(grp == 0)
                def _():
                    fringe_copy(k, end_to).wait_recv()
                    blend(k, fin, out_ref)

    for condition, item in pending:
        if condition is None:
            item.wait_send()
        else:
            pl.when(condition)(item.wait_send)


def per_device(velocity, fringe_columns):
    _, comps, _, rows_all, cols_all = velocity.shape
    n_xy, n_gz = lax.axis_size("xy"), lax.axis_size("gz")
    cross = rows_all * n_xy
    delta = (2.0 * math.pi / cols_all * (2.0 * math.pi / cross) * level_gap) ** (1.0 / 3.0)
    width = fringe_columns.shape[0]
    half = cols_all // 2
    along = derivative_matrix(cols_all).T
    same, other = along[:half, :half], along[half:, :half]
    mx = np.concatenate([two_parts((same + other) / 2), two_parts((same - other) / 2)])
    across = derivative_matrix(cross)
    my = two_parts(across[:rows_all, :rows_all])
    if n_xy > 1:
        spread, gather = factored(across[rows_all:, :rows_all])
    else:
        spread, gather = np.zeros((rows_all, 16)), np.zeros((16, rows_all))
    rank = gather.shape[0]
    gather = two_parts(gather)
    spread = two_parts(spread).reshape(2, -1, rows_all, rank)
    others = spread.shape[1]
    offsets = np.arange(width)
    weights = (0.5 * (1.0 + np.cos(np.pi * offsets / width))).astype(np.float32)[None]
    plane = (comps, rows_all, cols_all)
    fringe = (comps, rows_all, width)
    copies = STEPS * CHUNKS * 5 + 2 * CHUNKS + 2 * STEPS * others
    vmem = pl.BlockSpec(memory_space=pltpu.VMEM)

    def buffer(*shape):
        return pltpu.VMEM(shape, jnp.float32)

    result = pl.pallas_call(
        functools.partial(kernel, (n_gz, n_xy, width, (smag_coeff * delta) ** 2)),
        out_shape=jax.ShapeDtypeStruct(plane, jnp.float32),
        in_specs=[vmem] * 7,
        out_specs=vmem,
        scratch_shapes=[
            buffer(STEPS, *plane),
            buffer(*plane),
            buffer(*plane),
            buffer(STEPS, 2, *plane),
            buffer(STEPS, 2, *plane),
            buffer(*plane),
            buffer(*plane),
            buffer(*plane),
            buffer(*plane),
            buffer(*plane),
            buffer(STEPS, *plane),
            buffer(2 * STEPS, comps, rank, cols_all),
            buffer(2 * STEPS, others, comps, rank, cols_all),
            buffer(STEPS, *fringe),
            buffer(STEPS, *fringe),
            pltpu.SemaphoreType.DMA((copies,)),
            pltpu.SemaphoreType.DMA((copies,)),
        ],
        compiler_params=pltpu.CompilerParams(
            collective_id=0, has_side_effects=True, vmem_limit_bytes=56 * 1024 * 1024
        ),
    )(
        velocity.reshape(plane), fringe_columns.reshape(1, width), jnp.asarray(weights),
        jnp.asarray(mx), jnp.asarray(my), jnp.asarray(gather), jnp.asarray(spread),
    )
    return result.reshape(velocity.shape)


def solution(mesh):
    in_specs = (P("grp", None, "gz", "xy", None), P())
    out_specs = P("grp", None, "gz", "xy", None)
    return jax.shard_map(
        per_device, mesh=mesh, in_specs=in_specs, out_specs=out_specs, check_vma=False
    )
```

```python
import functools
import math

import jax
import jax.numpy as jnp
import ml_dtypes
import numpy as np
from jax import lax
from jax.experimental import pallas as pl
from jax.experimental.pallas import tpu as pltpu
from jax.sharding import PartitionSpec as P

STEPS = 2
CHUNKS = 4
ROWS = 8

time_step = 0.001
level_gap = 0.05
smag_coeff = 0.16
MESH = pl.DeviceIdType.MESH


def derivative_matrix(points):
    offsets = np.arange(points)
    distance = offsets[:, None] - offsets[None, :]
    safe = np.where(distance == 0, 1, distance)
    entries = 0.5 * (1.0 - 2.0 * (distance % 2)) / np.tan(np.pi * safe / points)
    return np.where(distance == 0, 0.0, entries)


def two_parts(matrix):
    single = matrix.astype(np.float32)
    high = single.astype(ml_dtypes.bfloat16)
    low = (single - high.astype(np.float32)).astype(ml_dtypes.bfloat16)
    return np.stack([high, low])


def factored(block):
    rest = block.copy()
    limit = np.abs(block).max() * 2.0**-30
    columns, rows = [], []
    while len(rows) < block.shape[1]:
        row, column = np.unravel_index(np.argmax(np.abs(rest)), rest.shape)
        if abs(rest[row, column]) < limit and len(rows) % 16 == 0:
            break
        if rest[row, column] == 0.0:
            columns.append(np.zeros_like(rest[:, 0]))
            rows.append(np.zeros_like(rest[0]))
            continue
        columns.append(rest[:, column] / rest[row, column])
        rows.append(rest[row].copy())
        rest = rest - np.outer(columns[-1], rows[-1])
    return np.stack(columns, axis=1), np.stack(rows, axis=0)


def halves(value):
    high = value.astype(jnp.bfloat16)
    return high, (value - high.astype(jnp.float32)).astype(jnp.bfloat16)


def dot(left, right):
    return jnp.dot(left, right, preferred_element_type=jnp.float32)


def dot_parts(left, right):
    return dot(left[0], right[0]) + (dot(left[0], right[1]) + dot(left[1], right[0]))


def kernel(
    sizes, in_ref, cols_ref, weight_ref, mx_ref, my_ref, gather_ref, spread_ref, out_ref,
    vel, ret, fin, vhalo, shalo, gx, gy, tend, sx, sy, sz, gsend, grecv, psend, precv,
    send_sem, recv_sem,
):
    n_gz, n_xy, width, scale = sizes
    _, rows_all, cols_all = in_ref.shape
    half = cols_all // 2
    chunk = rows_all // CHUNKS
    grp, gz, xy = lax.axis_index("grp"), lax.axis_index("gz"), lax.axis_index("xy")
    domain = lax.rem(gz, 2)
    pair = gz - domain
    level = pair + grp
    levels = n_gz
    swapped = domain != grp
    has_up = level < levels - 1
    has_down = level > 0
    is_farm = domain == 0

    def at_level(other):
        other = lax.rem(other + levels, levels)
        parity = lax.rem(other, 2)
        return (parity, other - parity + domain, xy)

    up, down = at_level(level + 1), at_level(level - 1)
    swap_to = (domain, pair + grp, xy)
    mid_to = (grp, pair + 1 - domain, xy)
    end_to = (1 - grp, gz, xy)

    def xy_to(offset):
        return (grp, gz, lax.rem(xy + offset, n_xy))

    bases = {}

    def copy(name, index, source, target, device):
        slot = bases.setdefault(name, len(bases) * 3 * CHUNKS) + index
        return pltpu.make_async_remote_copy(
            src_ref=source, dst_ref=target, send_sem=send_sem.at[slot],
            recv_sem=recv_sem.at[slot], device_id=device, device_id_type=MESH,
        )

    def when(condition, action):
        if condition is None:
            action()
        else:
            pl.when(condition)(action)

    def part(ref, k):
        return ref.at[pl.ds(k * chunk, chunk), :]

    def each(body):
        def step(c, carry):
            body(c)
            return carry

        lax.fori_loop(0, 3, step, 0)

    def flush(*waits):
        def body(c):
            for condition, copies in waits:
                def wait():
                    for item in copies(c):
                        item.wait_send()

                when(condition, wait)

        each(body)

    barrier = pltpu.get_barrier_semaphore()
    for device in [up, down, mid_to, end_to] + [xy_to(o) for o in range(1, n_xy)]:
        pl.semaphore_signal(barrier, inc=1, device_id=device, device_id_type=MESH)

    @pl.when(swapped)
    def _():
        pl.semaphore_signal(barrier, inc=1, device_id=swap_to, device_id_type=MESH)
        pl.semaphore_wait(barrier, 4 + n_xy)

    @pl.when(jnp.logical_not(swapped))
    def _():
        pl.semaphore_wait(barrier, 3 + n_xy)

    def z_copy(kind, s, c, k, upward):
        source, halo = (vel, vhalo) if kind == "v" else (sz, shalo)
        side, device = (0, up) if upward else (1, down)
        return copy(
            (kind, s, side), c * CHUNKS + k, part(source.at[s, c], k), part(halo.at[s, side, c], k), device
        )

    def z_start(kind, s, c, k):
        pl.when(has_up)(z_copy(kind, s, c, k, True).start)
        pl.when(has_down)(z_copy(kind, s, c, k, False).start)

    def z_wait(kind, s, components, k):
        def wait(upward):
            for c in components:
                z_copy(kind, s, c, k, upward).wait_recv()

        pl.when(has_down)(lambda: wait(True))
        pl.when(has_up)(lambda: wait(False))

    def z_flush(kind, s):
        return [
            (has_up, lambda c: [z_copy(kind, s, c, k, True) for k in range(CHUNKS)]),
            (has_down, lambda c: [z_copy(kind, s, c, k, False) for k in range(CHUNKS)]),
        ]

    def swap_in(c, k):
        return copy("in", c * CHUNKS + k, part(in_ref.at[c], k), part(vel.at[0, c], k), swap_to)

    def swap_back(c, k):
        return copy("out", c * CHUNKS + k, part(ret.at[c], k), part(fin.at[c], k), swap_to)

    def fringe_copy(s, c, k):
        device = end_to if s == STEPS - 1 else mid_to
        return copy(("f", s), c * CHUNKS + k, part(psend.at[s, c], k), part(precv.at[s, c], k), device)

    def g_copy(index, o, c):
        return copy(("g", index, o), c, gsend.at[index, c], grecv.at[index, o - 1, c], xy_to(o))

    @pl.when(swapped)
    def _():
        def body(c):
            for k in range(CHUNKS):
                swap_in(c, k).start()

        each(body)

    @pl.when(jnp.logical_not(swapped))
    def _():
        vel[0] = in_ref[...]

    @pl.when(level == 0)
    def _():
        for s in range(STEPS):
            vhalo[s, 0] = jnp.zeros_like(vel[0])
            shalo[s, 0] = jnp.zeros_like(vel[0])

    @pl.when(level == levels - 1)
    def _():
        for s in range(STEPS):
            vhalo[s, 1] = jnp.zeros_like(vel[0])
            shalo[s, 1] = jnp.zeros_like(vel[0])

    picker = jnp.where(
        lax.broadcasted_iota(jnp.int32, (cols_all, width), 0) == cols_ref[...], 1.0, 0.0
    ).astype(jnp.bfloat16)

    def picked(field):
        high = field.astype(jnp.bfloat16)
        rest = field - high.astype(jnp.float32)
        middle = rest.astype(jnp.bfloat16)
        low = (rest - middle.astype(jnp.float32)).astype(jnp.bfloat16)
        return (dot(high, picker) + (dot(middle, picker) + dot(low, picker))) * weight_ref[...]

    def x_derived(field):
        left, right = field[:, :half], field[:, half:]
        total = dot_parts(halves(left + right), (mx_ref[0], mx_ref[1]))
        difference = dot_parts(halves(left - right), (mx_ref[2], mx_ref[3]))
        return jnp.concatenate([total + difference, total - difference], axis=1)

    def compress(index, c, field):
        gsend[index, c] = dot_parts((gather_ref[0], gather_ref[1]), field)
        for o in range(1, n_xy):
            g_copy(index, o, c).start()

    def received(index, c):
        result = None
        for o in range(1, n_xy):
            g_copy(index, o, c).wait_recv()
            term = dot_parts((spread_ref[0, o - 1], spread_ref[1, o - 1]), halves(grecv[index, o - 1, c]))
            result = term if result is None else result + term
        return result

    def g_flush(index):
        return (None, lambda c: [g_copy(index, o, c) for o in range(1, n_xy)])

    def derive(s, c):
        field = vel[s, c]
        parts = halves(field)
        compress(2 * s, c, parts)
        gy[c] = dot_parts((my_ref[0], my_ref[1]), parts)
        gx[c] = x_derived(field)

    z_scale = 1.0 / (2.0 * level_gap)

    def arrive(c):
        for k in range(CHUNKS):
            pl.when(swapped)(swap_in(c, k).wait_recv)
            z_start("v", 0, c, k)
        derive(0, c)

    each(arrive)

    for s in range(STEPS):
        last = s == STEPS - 1

        def second(c):
            if n_xy > 1:
                gy[c] = gy[c] + received(2 * s, c)

        each(second)

        def pointwise(i, carry):
            rows = pl.ds(pl.multiple_of(i * ROWS, ROWS), ROWS)
            u = [vel[s, c, rows, :] for c in range(3)]
            dx = [gx[c, rows, :] for c in range(3)]
            dy = [gy[c, rows, :] for c in range(3)]
            dz = [(vhalo[s, 1, c, rows, :] - vhalo[s, 0, c, rows, :]) * z_scale for c in range(3)]
            for c in range(3):
                tend[c, rows, :] = -(u[0] * dx[c] + u[1] * dy[c] + u[2] * dz[c])
            xx, yy, zz = dx[0], dy[1], dz[2]
            xy_, xz, yz = 0.5 * (dy[0] + dx[1]), 0.5 * (dz[0] + dx[2]), 0.5 * (dz[1] + dy[2])
            total = xx * xx + yy * yy + zz * zz + 2.0 * (xy_ * xy_ + xz * xz + yz * yz)
            eddy = (2.0 * scale) * jnp.sqrt(2.0 * total)
            xy_, xz, yz = eddy * xy_, eddy * xz, eddy * yz
            sx[0, rows, :] = eddy * xx
            sx[1, rows, :] = xy_
            sx[2, rows, :] = xz
            sy[0, rows, :] = xy_
            sy[1, rows, :] = eddy * yy
            sy[2, rows, :] = yz
            sz[s, 0, rows, :] = xz
            sz[s, 1, rows, :] = yz
            sz[s, 2, rows, :] = eddy * zz
            return carry

        for k in range(CHUNKS):
            z_wait("v", s, range(3), k)
            lax.fori_loop(k * chunk // ROWS, (k + 1) * chunk // ROWS, pointwise, 0)
            z_start("s", s, 0, k)
        for c in (1, 2):
            for k in range(CHUNKS):
                z_start("s", s, c, k)

        def third(c):
            parts = halves(sy[c])
            compress(2 * s + 1, c, parts)
            tend[c] = tend[c] + (x_derived(sx[c]) + dot_parts((my_ref[0], my_ref[1]), parts))

        each(third)

        def fourth(c):
            if n_xy > 1:
                tend[c] = tend[c] + received(2 * s + 1, c)

        each(fourth)
        flush(*z_flush("v", s), g_flush(2 * s), g_flush(2 * s + 1))

        def update(c, k, target):
            z_wait("s", s, [c], k)
            rows = pl.ds(k * chunk, chunk)
            along_z = (shalo[s, 1, c, rows, :] - shalo[s, 0, c, rows, :]) * z_scale
            target[c, rows, :] = vel[s, c, rows, :] + time_step * (tend[c, rows, :] + along_z)

        def pick(c, k, source):
            rows = pl.ds(k * chunk, chunk)
            psend[s, c, rows, :] = picked(source[c, rows, :])
            fringe_copy(s, c, k).start()

        def blend(c, k, source, target):
            fringe_copy(s, c, k).wait_recv()
            rows = pl.ds(k * chunk, chunk)
            own = source[c, rows, :width] * (1.0 - weight_ref[...])
            target[c, rows, :width] = own + precv[s, c, rows, :]

        if not last:
            following = vel.at[s + 1]

            def advance(c):
                for k in range(CHUNKS):
                    update(c, k, following)

                    @pl.when(jnp.logical_not(is_farm))
                    def _():
                        pick(c, k, following)
                        z_start("v", s + 1, c, k)

                @pl.when(is_farm)
                def _():
                    for k in range(CHUNKS):
                        blend(c, k, following, following)
                        z_start("v", s + 1, c, k)

                derive(s + 1, c)

            each(advance)
            flush(*z_flush("s", s))
        else:
            def finish(c):
                for k in range(CHUNKS):
                    pl.when(swapped)(swap_back(c, k).wait_recv)
                    pl.when(grp == 1)(lambda: pick(c, k, fin))
                    rows = pl.ds(k * chunk, chunk)
                    out_ref[c, rows, :] = fin[c, rows, :]

                @pl.when(grp == 0)
                def _():
                    for k in range(CHUNKS):
                        blend(c, k, fin, out_ref)

            def advance(c):
                for k in range(CHUNKS):
                    @pl.when(swapped)
                    def _():
                        update(c, k, ret)
                        swap_back(c, k).start()

                    pl.when(jnp.logical_not(swapped))(lambda: update(c, k, fin))

                pl.when(c > 0)(lambda: finish(c - 1))

            each(advance)
            finish(2)
            flush(
                *z_flush("s", s),
                (swapped, lambda c: [swap_in(c, k) for k in range(CHUNKS)]),
                (swapped, lambda c: [swap_back(c, k) for k in range(CHUNKS)]),
                (grp == 1, lambda c: [fringe_copy(s, c, k) for k in range(CHUNKS)]),
                *[
                    (jnp.logical_not(is_farm), lambda c, t=t: [fringe_copy(t, c, k) for k in range(CHUNKS)])
                    for t in range(STEPS - 1)
                ],
            )


def per_device(velocity, fringe_columns):
    _, comps, _, rows_all, cols_all = velocity.shape
    n_xy, n_gz = lax.axis_size("xy"), lax.axis_size("gz")
    cross = rows_all * n_xy
    delta = (2.0 * math.pi / cols_all * (2.0 * math.pi / cross) * level_gap) ** (1.0 / 3.0)
    width = fringe_columns.shape[0]
    half = cols_all // 2
    along = derivative_matrix(cols_all).T
    same, other = along[:half, :half], along[half:, :half]
    mx = np.concatenate([two_parts((same + other) / 2), two_parts((same - other) / 2)])
    across = derivative_matrix(cross)
    my = two_parts(across[:rows_all, :rows_all])
    if n_xy > 1:
        spread, gather = factored(across[rows_all:, :rows_all])
    else:
        spread, gather = np.zeros((rows_all, 16)), np.zeros((16, rows_all))
    rank = gather.shape[0]
    gather = two_parts(gather)
    spread = two_parts(spread).reshape(2, -1, rows_all, rank)
    others = spread.shape[1]
    offsets = np.arange(width)
    weights = (0.5 * (1.0 + np.cos(np.pi * offsets / width))).astype(np.float32)[None]
    plane = (comps, rows_all, cols_all)
    fringe = (comps, rows_all, width)
    copies = 3 * CHUNKS * (STEPS * 5 + 2 + 2 * STEPS * others)
    vmem = pl.BlockSpec(memory_space=pltpu.VMEM)

    def buffer(*shape):
        return pltpu.VMEM(shape, jnp.float32)

    result = pl.pallas_call(
        functools.partial(kernel, (n_gz, n_xy, width, (smag_coeff * delta) ** 2)),
        out_shape=jax.ShapeDtypeStruct(plane, jnp.float32),
        in_specs=[vmem] * 7,
        out_specs=vmem,
        scratch_shapes=[
            buffer(STEPS, *plane),
            buffer(*plane),
            buffer(*plane),
            buffer(STEPS, 2, *plane),
            buffer(STEPS, 2, *plane),
            buffer(*plane),
            buffer(*plane),
            buffer(*plane),
            buffer(*plane),
            buffer(*plane),
            buffer(STEPS, *plane),
            buffer(2 * STEPS, comps, rank, cols_all),
            buffer(2 * STEPS, others, comps, rank, cols_all),
            buffer(STEPS, *fringe),
            buffer(STEPS, *fringe),
            pltpu.SemaphoreType.DMA((copies,)),
            pltpu.SemaphoreType.DMA((copies,)),
        ],
        compiler_params=pltpu.CompilerParams(
            collective_id=0, has_side_effects=True, vmem_limit_bytes=56 * 1024 * 1024
        ),
    )(
        velocity.reshape(plane), fringe_columns.reshape(1, width), jnp.asarray(weights),
        jnp.asarray(mx), jnp.asarray(my), jnp.asarray(gather), jnp.asarray(spread),
    )
    return result.reshape(velocity.shape)


def solution(mesh):
    in_specs = (P("grp", None, "gz", "xy", None), P())
    out_specs = P("grp", None, "gz", "xy", None)
    return jax.shard_map(
        per_device, mesh=mesh, in_specs=in_specs, out_specs=out_specs, check_vma=False
    )
```

```python
import functools
import math

import jax
import jax.numpy as jnp
import ml_dtypes
import numpy as np
from jax import lax
from jax.experimental import pallas as pl
from jax.experimental.pallas import tpu as pltpu
from jax.sharding import PartitionSpec as P

STEPS = 2
CHUNKS = 4
ROWS = 8
BLOCK = 256

time_step = 0.001
level_gap = 0.05
smag_coeff = 0.16
MESH = pl.DeviceIdType.MESH


def derivative_matrix(points):
    offsets = np.arange(points)
    distance = offsets[:, None] - offsets[None, :]
    safe = np.where(distance == 0, 1, distance)
    entries = 0.5 * (1.0 - 2.0 * (distance % 2)) / np.tan(np.pi * safe / points)
    return np.where(distance == 0, 0.0, entries)


def two_parts(matrix):
    single = matrix.astype(np.float32)
    high = single.astype(ml_dtypes.bfloat16)
    low = (single - high.astype(np.float32)).astype(ml_dtypes.bfloat16)
    return np.stack([high, low])


def factored(block):
    rest = block.copy()
    limit = np.abs(block).max() * 2.0**-30
    columns, rows = [], []
    while len(rows) < block.shape[1]:
        row, column = np.unravel_index(np.argmax(np.abs(rest)), rest.shape)
        if abs(rest[row, column]) < limit and len(rows) % 16 == 0:
            break
        if rest[row, column] == 0.0:
            columns.append(np.zeros_like(rest[:, 0]))
            rows.append(np.zeros_like(rest[0]))
            continue
        columns.append(rest[:, column] / rest[row, column])
        rows.append(rest[row].copy())
        rest = rest - np.outer(columns[-1], rows[-1])
    return np.stack(columns, axis=1), np.stack(rows, axis=0)


def halves(value):
    high = value.astype(jnp.bfloat16)
    return high, (value - high.astype(jnp.float32)).astype(jnp.bfloat16)


def dot(left, right):
    return jnp.dot(left, right, preferred_element_type=jnp.float32)


def kernel(
    sizes, in_ref, cols_ref, weight_ref, mx_ref, my_ref, spread_ref, out_ref,
    vel, ret, fin, vhalo, shalo, gx, gy, tend, sx, sy, sz, gsend, grecv, psend, precv,
    send_sem, recv_sem,
):
    n_gz, n_xy, width, scale = sizes
    _, rows_all, cols_all = in_ref.shape
    half = cols_all // 2
    chunk = rows_all // CHUNKS
    grp, gz, xy = lax.axis_index("grp"), lax.axis_index("gz"), lax.axis_index("xy")
    domain = lax.rem(gz, 2)
    pair = gz - domain
    level = pair + grp
    levels = n_gz
    swapped = domain != grp
    has_up = level < levels - 1
    has_down = level > 0
    is_farm = domain == 0

    def at_level(other):
        other = lax.rem(other + levels, levels)
        parity = lax.rem(other, 2)
        return (parity, other - parity + domain, xy)

    up, down = at_level(level + 1), at_level(level - 1)
    swap_to = (domain, pair + grp, xy)
    mid_to = (grp, pair + 1 - domain, xy)
    end_to = (1 - grp, gz, xy)

    def xy_to(offset):
        return (grp, gz, lax.rem(xy + offset, n_xy))

    bases = {}

    def copy(name, index, source, target, device):
        slot = bases.setdefault(name, len(bases) * 3 * CHUNKS) + index
        return pltpu.make_async_remote_copy(
            src_ref=source, dst_ref=target, send_sem=send_sem.at[slot],
            recv_sem=recv_sem.at[slot], device_id=device, device_id_type=MESH,
        )

    def when(condition, action):
        if condition is None:
            action()
        else:
            pl.when(condition)(action)

    def part(ref, k):
        return ref.at[pl.ds(k * chunk, chunk), :]

    def each(body):
        def step(c, carry):
            body(c)
            return carry

        lax.fori_loop(0, 3, step, 0)

    def flush(*waits):
        def body(c):
            for condition, copies in waits:
                def wait():
                    for item in copies(c):
                        item.wait_send()

                when(condition, wait)

        each(body)

    barrier = pltpu.get_barrier_semaphore()
    for device in [up, down, mid_to, end_to] + [xy_to(o) for o in range(1, n_xy)]:
        pl.semaphore_signal(barrier, inc=1, device_id=device, device_id_type=MESH)

    @pl.when(swapped)
    def _():
        pl.semaphore_signal(barrier, inc=1, device_id=swap_to, device_id_type=MESH)
        pl.semaphore_wait(barrier, 4 + n_xy)

    @pl.when(jnp.logical_not(swapped))
    def _():
        pl.semaphore_wait(barrier, 3 + n_xy)

    def z_copy(kind, s, c, k, upward):
        source, halo = (vel, vhalo) if kind == "v" else (sz, shalo)
        side, device = (0, up) if upward else (1, down)
        return copy(
            (kind, s, side), c * CHUNKS + k, part(source.at[s, c], k), part(halo.at[s, side, c], k), device
        )

    def z_start(kind, s, c, k):
        pl.when(has_up)(z_copy(kind, s, c, k, True).start)
        pl.when(has_down)(z_copy(kind, s, c, k, False).start)

    def z_wait(kind, s, components, k):
        def wait(upward):
            for c in components:
                z_copy(kind, s, c, k, upward).wait_recv()

        pl.when(has_down)(lambda: wait(True))
        pl.when(has_up)(lambda: wait(False))

    def z_flush(kind, s):
        return [
            (has_up, lambda c: [z_copy(kind, s, c, k, True) for k in range(CHUNKS)]),
            (has_down, lambda c: [z_copy(kind, s, c, k, False) for k in range(CHUNKS)]),
        ]

    def swap_in(c, k):
        return copy("in", c * CHUNKS + k, part(in_ref.at[c], k), part(vel.at[0, c], k), swap_to)

    def swap_back(c, k):
        return copy("out", c * CHUNKS + k, part(ret.at[c], k), part(fin.at[c], k), swap_to)

    def fringe_copy(s, c, k):
        device = end_to if s == STEPS - 1 else mid_to
        return copy(("f", s), c * CHUNKS + k, part(psend.at[s, c], k), part(precv.at[s, c], k), device)

    def g_copy(index, o, c):
        return copy(("g", index, o), c, gsend.at[index, c], grecv.at[index, o - 1, c], xy_to(o))

    @pl.when(swapped)
    def _():
        def body(c):
            for k in range(CHUNKS):
                swap_in(c, k).start()

        each(body)

    @pl.when(jnp.logical_not(swapped))
    def _():
        vel[0] = in_ref[...]

    @pl.when(level == 0)
    def _():
        for s in range(STEPS):
            vhalo[s, 0] = jnp.zeros_like(vel[0])
            shalo[s, 0] = jnp.zeros_like(vel[0])

    @pl.when(level == levels - 1)
    def _():
        for s in range(STEPS):
            vhalo[s, 1] = jnp.zeros_like(vel[0])
            shalo[s, 1] = jnp.zeros_like(vel[0])

    picker = jnp.where(
        lax.broadcasted_iota(jnp.int32, (cols_all, width), 0) == cols_ref[...], 1.0, 0.0
    ).astype(jnp.bfloat16)

    def picked(field):
        high = field.astype(jnp.bfloat16)
        rest = field - high.astype(jnp.float32)
        middle = rest.astype(jnp.bfloat16)
        low = (rest - middle.astype(jnp.float32)).astype(jnp.bfloat16)
        wide = dot(jnp.concatenate([high, middle, low], axis=0), picker)
        return (wide[:chunk] + (wide[chunk : 2 * chunk] + wide[2 * chunk :])) * weight_ref[...]

    def x_derived(field):
        left, right = field[:, :half], field[:, half:]
        both = []
        for at, value in ((0, left + right), (2, left - right)):
            high, low = halves(value)
            wide = dot(jnp.concatenate([high, low], axis=0), mx_ref[at])
            both.append(wide[:rows_all] + (wide[rows_all:] + dot(high, mx_ref[at + 1])))
        return jnp.concatenate([both[0] + both[1], both[0] - both[1]], axis=1)

    def y_derived(index, c, field):
        high, low = halves(field)
        lines = my_ref.shape[0] // 2
        wide = dot(my_ref[...], high)
        total = wide[:lines] + (wide[lines:] + dot(my_ref[:lines, :], low))
        gsend[index, c] = total[rows_all:]
        for o in range(1, n_xy):
            g_copy(index, o, c).start()
        return total[:rows_all]

    def received(index, c):
        result = None
        for o in range(1, n_xy):
            g_copy(index, o, c).wait_recv()
            high, low = halves(grecv[index, o - 1, c])
            term = dot(spread_ref[o - 1], jnp.concatenate([high, high, low], axis=0))
            result = term if result is None else result + term
        return result

    def g_flush(index):
        return (None, lambda c: [g_copy(index, o, c) for o in range(1, n_xy)])

    def derive(s, c):
        field = vel[s, c]
        gy[c] = y_derived(2 * s, c, field)
        gx[c] = x_derived(field)

    z_scale = 1.0 / (2.0 * level_gap)

    def arrive(c):
        for k in range(CHUNKS):
            pl.when(swapped)(swap_in(c, k).wait_recv)
            z_start("v", 0, c, k)
        derive(0, c)

    each(arrive)

    for s in range(STEPS):
        last = s == STEPS - 1

        def second(c):
            if n_xy > 1:
                gy[c] = gy[c] + received(2 * s, c)

        each(second)

        def pointwise(i, carry):
            for first in range(0, cols_all, BLOCK):
                block(pl.ds(pl.multiple_of(i * ROWS, ROWS), ROWS), pl.ds(first, BLOCK))
            return carry

        def block(rows, lanes):
            u = [vel[s, c, rows, lanes] for c in range(3)]
            dx = [gx[c, rows, lanes] for c in range(3)]
            dy = [gy[c, rows, lanes] for c in range(3)]
            dz = [(vhalo[s, 1, c, rows, lanes] - vhalo[s, 0, c, rows, lanes]) * z_scale for c in range(3)]
            for c in range(3):
                tend[c, rows, lanes] = -(u[0] * dx[c] + u[1] * dy[c] + u[2] * dz[c])
            xx, yy, zz = dx[0], dy[1], dz[2]
            xy_, xz, yz = 0.5 * (dy[0] + dx[1]), 0.5 * (dz[0] + dx[2]), 0.5 * (dz[1] + dy[2])
            total = xx * xx + yy * yy + zz * zz + 2.0 * (xy_ * xy_ + xz * xz + yz * yz)
            eddy = (2.0 * scale) * jnp.sqrt(2.0 * total)
            xy_, xz, yz = eddy * xy_, eddy * xz, eddy * yz
            sx[0, rows, lanes] = eddy * xx
            sx[1, rows, lanes] = xy_
            sx[2, rows, lanes] = xz
            sy[0, rows, lanes] = xy_
            sy[1, rows, lanes] = eddy * yy
            sy[2, rows, lanes] = yz
            sz[s, 0, rows, lanes] = xz
            sz[s, 1, rows, lanes] = yz
            sz[s, 2, rows, lanes] = eddy * zz

        for k in range(CHUNKS):
            z_wait("v", s, range(3), k)
            lax.fori_loop(k * chunk // ROWS, (k + 1) * chunk // ROWS, pointwise, 0)
            z_start("s", s, 0, k)
        for c in (1, 2):
            for k in range(CHUNKS):
                z_start("s", s, c, k)

        def third(c):
            tend[c] = tend[c] + y_derived(2 * s + 1, c, sy[c])
            tend[c] = tend[c] + x_derived(sx[c])

        each(third)

        def fourth(c):
            if n_xy > 1:
                tend[c] = tend[c] + received(2 * s + 1, c)

        each(fourth)
        flush(*z_flush("v", s), g_flush(2 * s), g_flush(2 * s + 1))

        def update(c, k, target):
            z_wait("s", s, [c], k)
            rows = pl.ds(k * chunk, chunk)
            along_z = (shalo[s, 1, c, rows, :] - shalo[s, 0, c, rows, :]) * z_scale
            target[c, rows, :] = vel[s, c, rows, :] + time_step * (tend[c, rows, :] + along_z)

        def pick(c, k, source):
            rows = pl.ds(k * chunk, chunk)
            psend[s, c, rows, :] = picked(source[c, rows, :])
            fringe_copy(s, c, k).start()

        def blend(c, k, source, target):
            fringe_copy(s, c, k).wait_recv()
            rows = pl.ds(k * chunk, chunk)
            own = source[c, rows, :width] * (1.0 - weight_ref[...])
            target[c, rows, :width] = own + precv[s, c, rows, :]

        if not last:
            following = vel.at[s + 1]

            def advance(c):
                for k in range(CHUNKS):
                    update(c, k, following)

                    @pl.when(jnp.logical_not(is_farm))
                    def _():
                        pick(c, k, following)
                        z_start("v", s + 1, c, k)

                @pl.when(is_farm)
                def _():
                    for k in range(CHUNKS):
                        blend(c, k, following, following)
                        z_start("v", s + 1, c, k)

                derive(s + 1, c)

            each(advance)
            flush(*z_flush("s", s))
        else:
            def finish(c):
                for k in range(CHUNKS):
                    pl.when(swapped)(swap_back(c, k).wait_recv)
                    pl.when(grp == 1)(lambda: pick(c, k, fin))
                    rows = pl.ds(k * chunk, chunk)
                    out_ref[c, rows, :] = fin[c, rows, :]

                @pl.when(grp == 0)
                def _():
                    for k in range(CHUNKS):
                        blend(c, k, fin, out_ref)

            def advance(c):
                for k in range(CHUNKS):
                    @pl.when(swapped)
                    def _():
                        update(c, k, ret)
                        swap_back(c, k).start()

                    pl.when(jnp.logical_not(swapped))(lambda: update(c, k, fin))

                pl.when(c > 0)(lambda: finish(c - 1))

            each(advance)
            finish(2)
            flush(
                *z_flush("s", s),
                (swapped, lambda c: [swap_in(c, k) for k in range(CHUNKS)]),
                (swapped, lambda c: [swap_back(c, k) for k in range(CHUNKS)]),
                (grp == 1, lambda c: [fringe_copy(s, c, k) for k in range(CHUNKS)]),
                *[
                    (jnp.logical_not(is_farm), lambda c, t=t: [fringe_copy(t, c, k) for k in range(CHUNKS)])
                    for t in range(STEPS - 1)
                ],
            )


def per_device(velocity, fringe_columns):
    _, comps, _, rows_all, cols_all = velocity.shape
    n_xy, n_gz = lax.axis_size("xy"), lax.axis_size("gz")
    cross = rows_all * n_xy
    delta = (2.0 * math.pi / cols_all * (2.0 * math.pi / cross) * level_gap) ** (1.0 / 3.0)
    width = fringe_columns.shape[0]
    half = cols_all // 2
    along = derivative_matrix(cols_all).T
    same, other = along[:half, :half], along[half:, :half]
    mx = np.concatenate([two_parts((same + other) / 2), two_parts((same - other) / 2)])
    across = derivative_matrix(cross)
    if n_xy > 1:
        spread, gather = factored(across[rows_all:, :rows_all])
    else:
        spread, gather = np.zeros((rows_all, 16)), np.zeros((16, rows_all))
    rank = gather.shape[0]
    my = np.concatenate(two_parts(np.concatenate([across[:rows_all, :rows_all], gather])))
    high, low = two_parts(spread)
    spread = np.concatenate([high, low, high], axis=1).reshape(-1, rows_all, 3 * rank)
    others = spread.shape[0]
    offsets = np.arange(width)
    weights = (0.5 * (1.0 + np.cos(np.pi * offsets / width))).astype(np.float32)[None]
    plane = (comps, rows_all, cols_all)
    fringe = (comps, rows_all, width)
    copies = 3 * CHUNKS * (STEPS * 5 + 2 + 2 * STEPS * others)
    vmem = pl.BlockSpec(memory_space=pltpu.VMEM)

    def buffer(*shape):
        return pltpu.VMEM(shape, jnp.float32)

    result = pl.pallas_call(
        functools.partial(kernel, (n_gz, n_xy, width, (smag_coeff * delta) ** 2)),
        out_shape=jax.ShapeDtypeStruct(plane, jnp.float32),
        in_specs=[vmem] * 6,
        out_specs=vmem,
        scratch_shapes=[
            buffer(STEPS, *plane),
            buffer(*plane),
            buffer(*plane),
            buffer(STEPS, 2, *plane),
            buffer(STEPS, 2, *plane),
            buffer(*plane),
            buffer(*plane),
            buffer(*plane),
            buffer(*plane),
            buffer(*plane),
            buffer(STEPS, *plane),
            buffer(2 * STEPS, comps, rank, cols_all),
            buffer(2 * STEPS, others, comps, rank, cols_all),
            buffer(STEPS, *fringe),
            buffer(STEPS, *fringe),
            pltpu.SemaphoreType.DMA((copies,)),
            pltpu.SemaphoreType.DMA((copies,)),
        ],
        compiler_params=pltpu.CompilerParams(
            collective_id=0, has_side_effects=True, vmem_limit_bytes=56 * 1024 * 1024
        ),
    )(
        velocity.reshape(plane), fringe_columns.reshape(1, width), jnp.asarray(weights),
        jnp.asarray(mx), jnp.asarray(my), jnp.asarray(spread),
    )
    return result.reshape(velocity.shape)


def solution(mesh):
    in_specs = (P("grp", None, "gz", "xy", None), P())
    out_specs = P("grp", None, "gz", "xy", None)
    return jax.shard_map(
        per_device, mesh=mesh, in_specs=in_specs, out_specs=out_specs, check_vma=False
    )
```

```python
import functools
import math

import jax
import jax.numpy as jnp
import ml_dtypes
import numpy as np
from jax import lax
from jax.experimental import pallas as pl
from jax.experimental.pallas import tpu as pltpu
from jax.sharding import PartitionSpec as P

STEPS = 2
CHUNKS = 2
ROWS = 8
BLOCK = 256

time_step = 0.001
level_gap = 0.05
smag_coeff = 0.16
MESH = pl.DeviceIdType.MESH


def derivative_matrix(points):
    offsets = np.arange(points)
    distance = offsets[:, None] - offsets[None, :]
    safe = np.where(distance == 0, 1, distance)
    entries = 0.5 * (1.0 - 2.0 * (distance % 2)) / np.tan(np.pi * safe / points)
    return np.where(distance == 0, 0.0, entries)


def two_parts(matrix):
    single = matrix.astype(np.float32)
    high = single.astype(ml_dtypes.bfloat16)
    low = (single - high.astype(np.float32)).astype(ml_dtypes.bfloat16)
    return np.stack([high, low])


def factored(block):
    rest = block.copy()
    limit = np.abs(block).max() * 2.0**-30
    columns, rows = [], []
    while len(rows) < block.shape[1]:
        row, column = np.unravel_index(np.argmax(np.abs(rest)), rest.shape)
        if abs(rest[row, column]) < limit and len(rows) % 16 == 0:
            break
        if rest[row, column] == 0.0:
            columns.append(np.zeros_like(rest[:, 0]))
            rows.append(np.zeros_like(rest[0]))
            continue
        columns.append(rest[:, column] / rest[row, column])
        rows.append(rest[row].copy())
        rest = rest - np.outer(columns[-1], rows[-1])
    return np.stack(columns, axis=1), np.stack(rows, axis=0)


def halves(value):
    high = value.astype(jnp.bfloat16)
    return high, (value - high.astype(jnp.float32)).astype(jnp.bfloat16)


def dot(left, right):
    return jnp.dot(left, right, preferred_element_type=jnp.float32)


def kernel(
    sizes, in_ref, cols_ref, weight_ref, mx_ref, my_ref, spread_ref, out_ref,
    vel, ret, fin, vhalo, shalo, gx, gy, tend, sx, sy, sz, gsend, grecv, psend, precv,
    send_sem, recv_sem,
):
    n_gz, n_xy, width, scale = sizes
    _, rows_all, cols_all = in_ref.shape
    half = cols_all // 2
    chunk = rows_all // CHUNKS
    grp, gz, xy = lax.axis_index("grp"), lax.axis_index("gz"), lax.axis_index("xy")
    domain = lax.rem(gz, 2)
    pair = gz - domain
    level = pair + grp
    levels = n_gz
    swapped = domain != grp
    has_up = level < levels - 1
    has_down = level > 0
    is_farm = domain == 0

    def at_level(other):
        other = lax.rem(other + levels, levels)
        parity = lax.rem(other, 2)
        return (parity, other - parity + domain, xy)

    up, down = at_level(level + 1), at_level(level - 1)
    swap_to = (domain, pair + grp, xy)
    mid_to = (grp, pair + 1 - domain, xy)
    end_to = (1 - grp, gz, xy)

    def xy_to(offset):
        return (grp, gz, lax.rem(xy + offset, n_xy))

    bases = {}

    def copy(name, index, source, target, device):
        slot = bases.setdefault(name, len(bases) * 3 * CHUNKS) + index
        return pltpu.make_async_remote_copy(
            src_ref=source, dst_ref=target, send_sem=send_sem.at[slot],
            recv_sem=recv_sem.at[slot], device_id=device, device_id_type=MESH,
        )

    def when(condition, action):
        if condition is None:
            action()
        else:
            pl.when(condition)(action)

    def part(ref, k):
        return ref.at[pl.ds(k[0] * chunk, k[1] * chunk), :]

    whole = [(0, CHUNKS)]
    split = [(k, 1) for k in range(CHUNKS)]

    def pieces(kind, s, c):
        if kind == "v":
            return split if c == 2 else whole
        return split if c == 0 or (c == 2 and s == STEPS - 1) else whole

    def ending(kind, s, c, k):
        return [piece for piece in pieces(kind, s, c) if piece[0] + piece[1] - 1 == k]

    def each(body):
        for c in range(3):
            body(c)

    def flush(*waits):
        for condition, copies in waits:
            def wait():
                for c in range(3):
                    for item in copies(c):
                        item.wait_send()

            when(condition, wait)

    barrier = pltpu.get_barrier_semaphore()
    for device in [up, down, mid_to, end_to] + [xy_to(o) for o in range(1, n_xy)]:
        pl.semaphore_signal(barrier, inc=1, device_id=device, device_id_type=MESH)

    @pl.when(swapped)
    def _():
        pl.semaphore_signal(barrier, inc=1, device_id=swap_to, device_id_type=MESH)
        pl.semaphore_wait(barrier, 4 + n_xy)

    @pl.when(jnp.logical_not(swapped))
    def _():
        pl.semaphore_wait(barrier, 3 + n_xy)

    def z_copy(kind, s, c, k, upward):
        source, halo = (vel, vhalo) if kind == "v" else (sz, shalo)
        side, device = (0, up) if upward else (1, down)
        return copy(
            (kind, s, side), c * CHUNKS + k[0], part(source.at[s, c], k), part(halo.at[s, side, c], k), device
        )

    def z_start(kind, s, c, k):
        pl.when(has_up)(z_copy(kind, s, c, k, True).start)
        pl.when(has_down)(z_copy(kind, s, c, k, False).start)

    def z_wait(kind, s, c, k):
        pl.when(has_down)(z_copy(kind, s, c, k, True).wait_recv)
        pl.when(has_up)(z_copy(kind, s, c, k, False).wait_recv)

    def z_flush(kind, s):
        return [
            (has_up, lambda c: [z_copy(kind, s, c, k, True) for k in pieces(kind, s, c)]),
            (has_down, lambda c: [z_copy(kind, s, c, k, False) for k in pieces(kind, s, c)]),
        ]

    def swap_in(c, k):
        return copy("in", c * CHUNKS + k[0], part(in_ref.at[c], k), part(vel.at[0, c], k), swap_to)

    def swap_back(c, k):
        return copy("out", c * CHUNKS + k[0], part(ret.at[c], k), part(fin.at[c], k), swap_to)

    def fringe_copy(s, c, k):
        device = end_to if s == STEPS - 1 else mid_to
        return copy(("f", s), c * CHUNKS + k[0], part(psend.at[s, c], k), part(precv.at[s, c], k), device)

    def g_copy(index, o, c):
        return copy(("g", index, o), c, gsend.at[index, c], grecv.at[index, o - 1, c], xy_to(o))

    @pl.when(swapped)
    def _():
        for c in range(3):
            for k in pieces("v", 0, c):
                swap_in(c, k).start()

    @pl.when(jnp.logical_not(swapped))
    def _():
        vel[0] = in_ref[...]

    @pl.when(level == 0)
    def _():
        for s in range(STEPS):
            vhalo[s, 0] = jnp.zeros_like(vel[0])
            shalo[s, 0] = jnp.zeros_like(vel[0])

    @pl.when(level == levels - 1)
    def _():
        for s in range(STEPS):
            vhalo[s, 1] = jnp.zeros_like(vel[0])
            shalo[s, 1] = jnp.zeros_like(vel[0])

    picker = jnp.where(
        lax.broadcasted_iota(jnp.int32, (cols_all, width), 0) == cols_ref[...], 1.0, 0.0
    ).astype(jnp.bfloat16)

    def picked(field):
        high = field.astype(jnp.bfloat16)
        rest = field - high.astype(jnp.float32)
        middle = rest.astype(jnp.bfloat16)
        low = (rest - middle.astype(jnp.float32)).astype(jnp.bfloat16)
        wide = dot(jnp.concatenate([high, middle, low], axis=0), picker)
        lines = field.shape[0]
        return (wide[:lines] + (wide[lines : 2 * lines] + wide[2 * lines :])) * weight_ref[...]

    def x_derived(field):
        left, right = field[:, :half], field[:, half:]
        both = []
        for at, value in ((0, left + right), (2, left - right)):
            high, low = halves(value)
            wide = dot(jnp.concatenate([high, low], axis=0), mx_ref[at])
            both.append(wide[:rows_all] + (wide[rows_all:] + dot(high, mx_ref[at + 1])))
        return jnp.concatenate([both[0] + both[1], both[0] - both[1]], axis=1)

    def y_derived(index, c, field):
        high, low = halves(field)
        lines = my_ref.shape[0] // 2
        wide = dot(my_ref[...], high)
        total = wide[:lines] + (wide[lines:] + dot(my_ref[:lines, :], low))
        gsend[index, c] = total[rows_all:]
        for o in range(1, n_xy):
            g_copy(index, o, c).start()
        return total[:rows_all]

    def received(index, c):
        result = None
        for o in range(1, n_xy):
            g_copy(index, o, c).wait_recv()
            high, low = halves(grecv[index, o - 1, c])
            term = dot(spread_ref[o - 1], jnp.concatenate([high, high, low], axis=0))
            result = term if result is None else result + term
        return result

    def g_flush(index):
        return (None, lambda c: [g_copy(index, o, c) for o in range(1, n_xy)])

    def derive(s, c):
        field = vel[s, c]
        gy[c] = y_derived(2 * s, c, field)
        gx[c] = x_derived(field)

    z_scale = 1.0 / (2.0 * level_gap)

    def arrive(c):
        for k in pieces("v", 0, c):
            pl.when(swapped)(swap_in(c, k).wait_recv)
            z_start("v", 0, c, k)
        derive(0, c)

    each(arrive)

    for s in range(STEPS):
        last = s == STEPS - 1

        def second(c):
            if n_xy > 1:
                gy[c] = gy[c] + received(2 * s, c)

        each(second)

        def pointwise(i, carry):
            for first in range(0, cols_all, BLOCK):
                block(pl.ds(pl.multiple_of(i * ROWS, ROWS), ROWS), pl.ds(first, BLOCK))
            return carry

        def block(rows, lanes):
            u = [vel[s, c, rows, lanes] for c in range(3)]
            dx = [gx[c, rows, lanes] for c in range(3)]
            dy = [gy[c, rows, lanes] for c in range(3)]
            dz = [(vhalo[s, 1, c, rows, lanes] - vhalo[s, 0, c, rows, lanes]) * z_scale for c in range(3)]
            for c in range(3):
                tend[c, rows, lanes] = -(u[0] * dx[c] + u[1] * dy[c] + u[2] * dz[c])
            xx, yy, zz = dx[0], dy[1], dz[2]
            xy_, xz, yz = 0.5 * (dy[0] + dx[1]), 0.5 * (dz[0] + dx[2]), 0.5 * (dz[1] + dy[2])
            total = xx * xx + yy * yy + zz * zz + 2.0 * (xy_ * xy_ + xz * xz + yz * yz)
            eddy = (2.0 * scale) * jnp.sqrt(2.0 * total)
            xy_, xz, yz = eddy * xy_, eddy * xz, eddy * yz
            sx[0, rows, lanes] = eddy * xx
            sx[1, rows, lanes] = xy_
            sx[2, rows, lanes] = xz
            sy[0, rows, lanes] = xy_
            sy[1, rows, lanes] = eddy * yy
            sy[2, rows, lanes] = yz
            sz[s, 0, rows, lanes] = xz
            sz[s, 1, rows, lanes] = yz
            sz[s, 2, rows, lanes] = eddy * zz

        for k in range(CHUNKS):
            for c in range(3):
                for piece in pieces("v", s, c):
                    if piece[0] == k:
                        z_wait("v", s, c, piece)
            lax.fori_loop(k * chunk // ROWS, (k + 1) * chunk // ROWS, pointwise, 0)
            for c in range(3):
                for piece in ending("s", s, c, k):
                    if c == 0:
                        z_start("s", s, c, piece)
        for c in (1, 2):
            for piece in pieces("s", s, c):
                z_start("s", s, c, piece)

        def third(c):
            tend[c] = tend[c] + y_derived(2 * s + 1, c, sy[c])
            tend[c] = tend[c] + x_derived(sx[c])

        each(third)

        def fourth(c):
            if n_xy > 1:
                tend[c] = tend[c] + received(2 * s + 1, c)

        each(fourth)
        flush(*z_flush("v", s), g_flush(2 * s), g_flush(2 * s + 1))

        def rows_of(k):
            return pl.ds(k[0] * chunk, k[1] * chunk)

        def update(c, k, target):
            z_wait("s", s, c, k)
            rows = rows_of(k)
            along_z = (shalo[s, 1, c, rows, :] - shalo[s, 0, c, rows, :]) * z_scale
            target[c, rows, :] = vel[s, c, rows, :] + time_step * (tend[c, rows, :] + along_z)

        def pick(c, k, source):
            psend[s, c, rows_of(k), :] = picked(source[c, rows_of(k), :])
            fringe_copy(s, c, k).start()

        def blend(c, k, source, target):
            fringe_copy(s, c, k).wait_recv()
            rows = rows_of(k)
            own = source[c, rows, :width] * (1.0 - weight_ref[...])
            target[c, rows, :width] = own + precv[s, c, rows, :]

        if not last:
            following = vel.at[s + 1]

            def advance(c):
                for k in pieces("s", s, c):
                    update(c, k, following)

                @pl.when(jnp.logical_not(is_farm))
                def _():
                    for k in pieces("v", s + 1, c):
                        pick(c, k, following)
                        z_start("v", s + 1, c, k)

                @pl.when(is_farm)
                def _():
                    for k in pieces("v", s + 1, c):
                        blend(c, k, following, following)
                        z_start("v", s + 1, c, k)

                derive(s + 1, c)

            each(advance)
            flush(*z_flush("s", s))
        else:
            def finish(c):
                for k in pieces("s", s, c):
                    pl.when(swapped)(swap_back(c, k).wait_recv)
                    pl.when(grp == 1)(lambda: pick(c, k, fin))
                    out_ref[c, rows_of(k), :] = fin[c, rows_of(k), :]

                @pl.when(grp == 0)
                def _():
                    for k in pieces("s", s, c):
                        blend(c, k, fin, out_ref)

            def advance(c):
                for k in pieces("s", s, c):
                    @pl.when(swapped)
                    def _():
                        update(c, k, ret)
                        swap_back(c, k).start()

                    pl.when(jnp.logical_not(swapped))(lambda: update(c, k, fin))

                if c > 0:
                    finish(c - 1)

            each(advance)
            finish(2)
            flush(
                *z_flush("s", s),
                (swapped, lambda c: [swap_in(c, k) for k in pieces("v", 0, c)]),
                (swapped, lambda c: [swap_back(c, k) for k in pieces("s", s, c)]),
                (grp == 1, lambda c: [fringe_copy(s, c, k) for k in pieces("s", s, c)]),
                *[
                    (
                        jnp.logical_not(is_farm),
                        lambda c, t=t: [fringe_copy(t, c, k) for k in pieces("v", t + 1, c)],
                    )
                    for t in range(STEPS - 1)
                ],
            )


def per_device(velocity, fringe_columns):
    _, comps, _, rows_all, cols_all = velocity.shape
    n_xy, n_gz = lax.axis_size("xy"), lax.axis_size("gz")
    cross = rows_all * n_xy
    delta = (2.0 * math.pi / cols_all * (2.0 * math.pi / cross) * level_gap) ** (1.0 / 3.0)
    width = fringe_columns.shape[0]
    half = cols_all // 2
    along = derivative_matrix(cols_all).T
    same, other = along[:half, :half], along[half:, :half]
    mx = np.concatenate([two_parts((same + other) / 2), two_parts((same - other) / 2)])
    across = derivative_matrix(cross)
    if n_xy > 1:
        spread, gather = factored(across[rows_all:, :rows_all])
    else:
        spread, gather = np.zeros((rows_all, 16)), np.zeros((16, rows_all))
    rank = gather.shape[0]
    my = np.concatenate(two_parts(np.concatenate([across[:rows_all, :rows_all], gather])))
    high, low = two_parts(spread)
    spread = np.concatenate([high, low, high], axis=1).reshape(-1, rows_all, 3 * rank)
    others = spread.shape[0]
    offsets = np.arange(width)
    weights = (0.5 * (1.0 + np.cos(np.pi * offsets / width))).astype(np.float32)[None]
    plane = (comps, rows_all, cols_all)
    fringe = (comps, rows_all, width)
    copies = 3 * CHUNKS * (STEPS * 5 + 2 + 2 * STEPS * others)
    vmem = pl.BlockSpec(memory_space=pltpu.VMEM)

    def buffer(*shape):
        return pltpu.VMEM(shape, jnp.float32)

    result = pl.pallas_call(
        functools.partial(kernel, (n_gz, n_xy, width, (smag_coeff * delta) ** 2)),
        out_shape=jax.ShapeDtypeStruct(plane, jnp.float32),
        in_specs=[vmem] * 6,
        out_specs=vmem,
        scratch_shapes=[
            buffer(STEPS, *plane),
            buffer(*plane),
            buffer(*plane),
            buffer(STEPS, 2, *plane),
            buffer(STEPS, 2, *plane),
            buffer(*plane),
            buffer(*plane),
            buffer(*plane),
            buffer(*plane),
            buffer(*plane),
            buffer(STEPS, *plane),
            buffer(2 * STEPS, comps, rank, cols_all),
            buffer(2 * STEPS, others, comps, rank, cols_all),
            buffer(STEPS, *fringe),
            buffer(STEPS, *fringe),
            pltpu.SemaphoreType.DMA((copies,)),
            pltpu.SemaphoreType.DMA((copies,)),
        ],
        compiler_params=pltpu.CompilerParams(
            collective_id=0, has_side_effects=True, vmem_limit_bytes=56 * 1024 * 1024
        ),
    )(
        velocity.reshape(plane), fringe_columns.reshape(1, width), jnp.asarray(weights),
        jnp.asarray(mx), jnp.asarray(my), jnp.asarray(spread),
    )
    return result.reshape(velocity.shape)


def solution(mesh):
    in_specs = (P("grp", None, "gz", "xy", None), P())
    out_specs = P("grp", None, "gz", "xy", None)
    return jax.shard_map(
        per_device, mesh=mesh, in_specs=in_specs, out_specs=out_specs, check_vma=False
    )
```

```python
import functools
import math

import jax
import jax.numpy as jnp
import ml_dtypes
import numpy as np
from jax import lax
from jax.experimental import pallas as pl
from jax.experimental.pallas import tpu as pltpu
from jax.sharding import PartitionSpec as P

STEPS = 2
CHUNKS = 8
PARTS = 2
ROWS = 16
BLOCK = 128

time_step = 0.001
level_gap = 0.05
smag_coeff = 0.16
MESH = pl.DeviceIdType.MESH


def derivative_matrix(points):
    offsets = np.arange(points)
    distance = offsets[:, None] - offsets[None, :]
    safe = np.where(distance == 0, 1, distance)
    entries = 0.5 * (1.0 - 2.0 * (distance % 2)) / np.tan(np.pi * safe / points)
    return np.where(distance == 0, 0.0, entries)


def two_parts(matrix):
    single = matrix.astype(np.float32)
    high = single.astype(ml_dtypes.bfloat16)
    low = (single - high.astype(np.float32)).astype(ml_dtypes.bfloat16)
    return np.stack([high, low])


def factored(block):
    rest = block.copy()
    limit = np.abs(block).max() * 2.0**-30
    columns, rows = [], []
    while len(rows) < block.shape[1]:
        row, column = np.unravel_index(np.argmax(np.abs(rest)), rest.shape)
        if abs(rest[row, column]) < limit and len(rows) % 16 == 0:
            break
        if rest[row, column] == 0.0:
            columns.append(np.zeros_like(rest[:, 0]))
            rows.append(np.zeros_like(rest[0]))
            continue
        columns.append(rest[:, column] / rest[row, column])
        rows.append(rest[row].copy())
        rest = rest - np.outer(columns[-1], rows[-1])
    return np.stack(columns, axis=1), np.stack(rows, axis=0)


def halves(value):
    high = value.astype(jnp.bfloat16)
    return high, (value - high.astype(jnp.float32)).astype(jnp.bfloat16)


def dot(left, right):
    return jnp.dot(left, right, preferred_element_type=jnp.float32)


def kernel(
    sizes, in_ref, cols_ref, weight_ref, mx_ref, my_ref, spread_ref, out_ref,
    vel, ret, fin, vhalo, shalo, gx, gy, tend, sx, sy, sz, gsend, grecv, psend, precv,
    send_sem, recv_sem,
):
    n_gz, n_xy, width, scale = sizes
    _, rows_all, cols_all = in_ref.shape
    half = cols_all // 2
    chunk = rows_all // CHUNKS
    step = min(ROWS, chunk)
    grp, gz, xy = lax.axis_index("grp"), lax.axis_index("gz"), lax.axis_index("xy")
    domain = lax.rem(gz, 2)
    pair = gz - domain
    level = pair + grp
    levels = n_gz
    swapped = domain != grp
    has_up = level < levels - 1
    has_down = level > 0
    is_farm = domain == 0

    def at_level(other):
        other = lax.rem(other + levels, levels)
        parity = lax.rem(other, 2)
        return (parity, other - parity + domain, xy)

    up, down = at_level(level + 1), at_level(level - 1)
    swap_to = (domain, pair + grp, xy)
    mid_to = (grp, pair + 1 - domain, xy)
    end_to = (1 - grp, gz, xy)

    def xy_to(offset):
        return (grp, gz, lax.rem(xy + offset, n_xy))

    slots = {}

    def copy(name, source, target, device):
        slot = slots.setdefault(name, len(slots))
        return pltpu.make_async_remote_copy(
            src_ref=source, dst_ref=target, send_sem=send_sem.at[slot],
            recv_sem=recv_sem.at[slot], device_id=device, device_id_type=MESH,
        )

    chunks = list(range(CHUNKS))
    parts = [(c, part) for c in range(3) for part in range(PARTS)]

    def region(ref, k):
        if isinstance(k, tuple):
            lines = rows_all // PARTS
            return ref.at[k[0], pl.ds(k[1] * lines, lines), :]
        return ref.at[:, pl.ds(k * chunk, chunk), :]

    def flush(condition, copies):
        def wait():
            for item in copies:
                item.wait_send()

        if condition is None:
            wait()
        else:
            pl.when(condition)(wait)

    barrier = pltpu.get_barrier_semaphore()
    for device in [up, down, mid_to, end_to] + [xy_to(o) for o in range(1, n_xy)]:
        pl.semaphore_signal(barrier, inc=1, device_id=device, device_id_type=MESH)

    @pl.when(swapped)
    def _():
        pl.semaphore_signal(barrier, inc=1, device_id=swap_to, device_id_type=MESH)
        pl.semaphore_wait(barrier, 4 + n_xy)

    @pl.when(jnp.logical_not(swapped))
    def _():
        pl.semaphore_wait(barrier, 3 + n_xy)

    def z_pieces(kind, s):
        return parts if kind == "v" and s == 0 else chunks

    def z_copy(kind, s, k, upward):
        source, halo = (vel, vhalo) if kind == "v" else (sz, shalo)
        side, device = (0, up) if upward else (1, down)
        return copy((kind, s, side, k), region(source.at[s], k), region(halo.at[s, side], k), device)

    def z_start(kind, s, k):
        pl.when(has_up)(z_copy(kind, s, k, True).start)
        pl.when(has_down)(z_copy(kind, s, k, False).start)

    def z_wait(kind, s, pieces):
        def wait(upward):
            for k in pieces:
                z_copy(kind, s, k, upward).wait_recv()

        pl.when(has_down)(lambda: wait(True))
        pl.when(has_up)(lambda: wait(False))

    def z_flush(kind, s):
        flush(has_up, [z_copy(kind, s, k, True) for k in z_pieces(kind, s)])
        flush(has_down, [z_copy(kind, s, k, False) for k in z_pieces(kind, s)])

    def swap_in(k):
        return copy(("in", k), region(in_ref, k), region(vel.at[0], k), swap_to)

    def swap_back(k):
        return copy(("out", k), region(ret, k), region(fin, k), swap_to)

    def fringe_copy(s, k):
        device = end_to if s == STEPS - 1 else mid_to
        return copy(("f", s, k), region(psend.at[s], k), region(precv.at[s], k), device)

    def g_copy(index, o, c):
        return copy(("g", index, o, c), gsend.at[index, c], grecv.at[index, o - 1, c], xy_to(o))

    @pl.when(swapped)
    def _():
        for k in parts:
            swap_in(k).start()

    @pl.when(jnp.logical_not(swapped))
    def _():
        vel[0] = in_ref[...]

    @pl.when(level == 0)
    def _():
        for s in range(STEPS):
            vhalo[s, 0] = jnp.zeros_like(vel[0])
            shalo[s, 0] = jnp.zeros_like(vel[0])

    @pl.when(level == levels - 1)
    def _():
        for s in range(STEPS):
            vhalo[s, 1] = jnp.zeros_like(vel[0])
            shalo[s, 1] = jnp.zeros_like(vel[0])

    picker = jnp.where(
        lax.broadcasted_iota(jnp.int32, (cols_all, width), 0) == cols_ref[...], 1.0, 0.0
    ).astype(jnp.bfloat16)

    def picked(field):
        high = field.astype(jnp.bfloat16)
        rest = field - high.astype(jnp.float32)
        middle = rest.astype(jnp.bfloat16)
        low = (rest - middle.astype(jnp.float32)).astype(jnp.bfloat16)
        wide = dot(jnp.concatenate([high, middle, low], axis=0), picker)
        lines = field.shape[0]
        return (wide[:lines] + (wide[lines : 2 * lines] + wide[2 * lines :])) * weight_ref[...]

    def x_derived(field):
        left, right = field[:, :half], field[:, half:]
        both = []
        for at, value in ((0, left + right), (2, left - right)):
            high, low = halves(value)
            wide = dot(jnp.concatenate([high, low], axis=0), mx_ref[at])
            both.append(wide[:rows_all] + (wide[rows_all:] + dot(high, mx_ref[at + 1])))
        return jnp.concatenate([both[0] + both[1], both[0] - both[1]], axis=1)

    def y_derived(index, c, field):
        high, low = halves(field)
        lines = my_ref.shape[0] // 2
        wide = dot(my_ref[...], high)
        total = wide[:lines] + (wide[lines:] + dot(my_ref[:lines, :], low))
        gsend[index, c] = total[rows_all:]
        for o in range(1, n_xy):
            g_copy(index, o, c).start()
        return total[:rows_all]

    def received(index, c):
        result = None
        for o in range(1, n_xy):
            g_copy(index, o, c).wait_recv()
            high, low = halves(grecv[index, o - 1, c])
            term = dot(spread_ref[o - 1], jnp.concatenate([high, high, low], axis=0))
            result = term if result is None else result + term
        return result

    def g_flush(index):
        flush(None, [g_copy(index, o, c) for o in range(1, n_xy) for c in range(3)])

    def derive(s, c):
        field = vel[s, c]
        gy[c] = y_derived(2 * s, c, field)
        gx[c] = x_derived(field)

    z_scale = 1.0 / (2.0 * level_gap)

    for c in range(3):
        for k in parts:
            if k[0] == c:
                pl.when(swapped)(swap_in(k).wait_recv)
                z_start("v", 0, k)
        derive(0, c)

    for s in range(STEPS):
        last = s == STEPS - 1
        if s > 0:
            for c in range(3):
                derive(s, c)
        if n_xy > 1:
            for c in range(3):
                gy[c] = gy[c] + received(2 * s, c)

        def pointwise(i, carry):
            for first in range(0, cols_all, BLOCK):
                block(pl.ds(pl.multiple_of(i * step, step), step), pl.ds(first, BLOCK))
            return carry

        def block(rows, lanes):
            u = [vel[s, c, rows, lanes] for c in range(3)]
            dx = [gx[c, rows, lanes] for c in range(3)]
            dy = [gy[c, rows, lanes] for c in range(3)]
            dz = [(vhalo[s, 1, c, rows, lanes] - vhalo[s, 0, c, rows, lanes]) * z_scale for c in range(3)]
            for c in range(3):
                tend[c, rows, lanes] = -(u[0] * dx[c] + u[1] * dy[c] + u[2] * dz[c])
            xx, yy, zz = dx[0], dy[1], dz[2]
            xy_, xz, yz = 0.5 * (dy[0] + dx[1]), 0.5 * (dz[0] + dx[2]), 0.5 * (dz[1] + dy[2])
            total = xx * xx + yy * yy + zz * zz + 2.0 * (xy_ * xy_ + xz * xz + yz * yz)
            eddy = (2.0 * scale) * jnp.sqrt(2.0 * total)
            xy_, xz, yz = eddy * xy_, eddy * xz, eddy * yz
            sx[0, rows, lanes] = eddy * xx
            sx[1, rows, lanes] = xy_
            sx[2, rows, lanes] = xz
            sy[0, rows, lanes] = xy_
            sy[1, rows, lanes] = eddy * yy
            sy[2, rows, lanes] = yz
            sz[s, 0, rows, lanes] = xz
            sz[s, 1, rows, lanes] = yz
            sz[s, 2, rows, lanes] = eddy * zz

        for k in chunks:
            if s > 0:
                z_wait("v", s, [k])
            elif k % (CHUNKS // PARTS) == 0:
                z_wait("v", s, [piece for piece in parts if piece[1] == k // (CHUNKS // PARTS)])
            lax.fori_loop(k * chunk // step, (k + 1) * chunk // step, pointwise, 0)
            z_start("s", s, k)

        for c in range(3):
            tend[c] = tend[c] + y_derived(2 * s + 1, c, sy[c])
            tend[c] = tend[c] + x_derived(sx[c])
        if n_xy > 1:
            for c in range(3):
                tend[c] = tend[c] + received(2 * s + 1, c)
        z_flush("v", s)
        g_flush(2 * s)
        g_flush(2 * s + 1)

        def update(k, target):
            rows = pl.ds(k * chunk, chunk)
            for c in range(3):
                along_z = (shalo[s, 1, c, rows, :] - shalo[s, 0, c, rows, :]) * z_scale
                target[c, rows, :] = vel[s, c, rows, :] + time_step * (tend[c, rows, :] + along_z)

        def pick(k, source):
            rows = pl.ds(k * chunk, chunk)
            fields = jnp.concatenate([source[c, rows, :] for c in range(3)], axis=0)
            values = picked(fields)
            for c in range(3):
                psend[s, c, rows, :] = values[c * chunk : (c + 1) * chunk]
            fringe_copy(s, k).start()

        def blend(k, source, target):
            fringe_copy(s, k).wait_recv()
            rows = pl.ds(k * chunk, chunk)
            for c in range(3):
                own = source[c, rows, :width] * (1.0 - weight_ref[...])
                target[c, rows, :width] = own + precv[s, c, rows, :]

        if not last:
            following = vel.at[s + 1]
            for k in chunks:
                z_wait("s", s, [k])
                update(k, following)

                @pl.when(jnp.logical_not(is_farm))
                def _():
                    pick(k, following)

                pl.when(is_farm)(lambda: blend(k, following, following))
                z_start("v", s + 1, k)
            z_flush("s", s)
            flush(jnp.logical_not(is_farm), [fringe_copy(s, k) for k in chunks])
        else:
            def finish(k):
                pl.when(swapped)(swap_back(k).wait_recv)
                pl.when(grp == 1)(lambda: pick(k, fin))
                rows = pl.ds(k * chunk, chunk)
                out_ref[:, rows, :] = fin[:, rows, :]
                pl.when(grp == 0)(lambda: blend(k, fin, out_ref))

            for k in chunks:
                z_wait("s", s, [k])

                @pl.when(swapped)
                def _():
                    update(k, ret)
                    swap_back(k).start()

                pl.when(jnp.logical_not(swapped))(lambda: update(k, fin))
                if k == 1:
                    flush(swapped, [swap_in(piece) for piece in parts])
                if k > 0:
                    finish(k - 1)
            finish(CHUNKS - 1)
            z_flush("s", s)
            flush(swapped, [swap_back(k) for k in chunks])
            flush(grp == 1, [fringe_copy(s, k) for k in chunks])


def per_device(velocity, fringe_columns):
    _, comps, _, rows_all, cols_all = velocity.shape
    n_xy, n_gz = lax.axis_size("xy"), lax.axis_size("gz")
    cross = rows_all * n_xy
    delta = (2.0 * math.pi / cols_all * (2.0 * math.pi / cross) * level_gap) ** (1.0 / 3.0)
    width = fringe_columns.shape[0]
    half = cols_all // 2
    along = derivative_matrix(cols_all).T
    same, other = along[:half, :half], along[half:, :half]
    mx = np.concatenate([two_parts((same + other) / 2), two_parts((same - other) / 2)])
    across = derivative_matrix(cross)
    if n_xy > 1:
        spread, gather = factored(across[rows_all:, :rows_all])
    else:
        spread, gather = np.zeros((rows_all, 16)), np.zeros((16, rows_all))
    rank = gather.shape[0]
    my = np.concatenate(two_parts(np.concatenate([across[:rows_all, :rows_all], gather])))
    high, low = two_parts(spread)
    spread = np.concatenate([high, low, high], axis=1).reshape(-1, rows_all, 3 * rank)
    others = spread.shape[0]
    offsets = np.arange(width)
    weights = (0.5 * (1.0 + np.cos(np.pi * offsets / width))).astype(np.float32)[None]
    plane = (comps, rows_all, cols_all)
    fringe = (comps, rows_all, width)
    copies = STEPS * (5 * CHUNKS + 6 * others) + CHUNKS + 9 * PARTS
    vmem = pl.BlockSpec(memory_space=pltpu.VMEM)

    def buffer(*shape):
        return pltpu.VMEM(shape, jnp.float32)

    result = pl.pallas_call(
        functools.partial(kernel, (n_gz, n_xy, width, (smag_coeff * delta) ** 2)),
        out_shape=jax.ShapeDtypeStruct(plane, jnp.float32),
        in_specs=[vmem] * 6,
        out_specs=vmem,
        scratch_shapes=[
            buffer(STEPS, *plane),
            buffer(*plane),
            buffer(*plane),
            buffer(STEPS, 2, *plane),
            buffer(STEPS, 2, *plane),
            buffer(*plane),
            buffer(*plane),
            buffer(*plane),
            buffer(*plane),
            buffer(*plane),
            buffer(STEPS, *plane),
            buffer(2 * STEPS, comps, rank, cols_all),
            buffer(2 * STEPS, others, comps, rank, cols_all),
            buffer(STEPS, *fringe),
            buffer(STEPS, *fringe),
            pltpu.SemaphoreType.DMA((copies,)),
            pltpu.SemaphoreType.DMA((copies,)),
        ],
        compiler_params=pltpu.CompilerParams(
            collective_id=0, has_side_effects=True, vmem_limit_bytes=56 * 1024 * 1024
        ),
    )(
        velocity.reshape(plane), fringe_columns.reshape(1, width), jnp.asarray(weights),
        jnp.asarray(mx), jnp.asarray(my), jnp.asarray(spread),
    )
    return result.reshape(velocity.shape)


def solution(mesh):
    in_specs = (P("grp", None, "gz", "xy", None), P())
    out_specs = P("grp", None, "gz", "xy", None)
    return jax.shard_map(
        per_device, mesh=mesh, in_specs=in_specs, out_specs=out_specs, check_vma=False
    )
```

```python
import functools
import math

import jax
import jax.numpy as jnp
import ml_dtypes
import numpy as np
from jax import lax
from jax.experimental import pallas as pl
from jax.experimental.pallas import tpu as pltpu
from jax.sharding import PartitionSpec as P

STEPS = 2
CHUNKS = 4
ROWS = 16
BLOCK = 128

time_step = 0.001
level_gap = 0.05
smag_coeff = 0.16
MESH = pl.DeviceIdType.MESH


def derivative_matrix(points):
    offsets = np.arange(points)
    distance = offsets[:, None] - offsets[None, :]
    safe = np.where(distance == 0, 1, distance)
    entries = 0.5 * (1.0 - 2.0 * (distance % 2)) / np.tan(np.pi * safe / points)
    return np.where(distance == 0, 0.0, entries)


def two_parts(matrix):
    single = matrix.astype(np.float32)
    high = single.astype(ml_dtypes.bfloat16)
    low = (single - high.astype(np.float32)).astype(ml_dtypes.bfloat16)
    return np.stack([high, low])


def factored(block):
    rest = block.copy()
    limit = np.abs(block).max() * 2.0**-30
    columns, rows = [], []
    while len(rows) < block.shape[1]:
        row, column = np.unravel_index(np.argmax(np.abs(rest)), rest.shape)
        if abs(rest[row, column]) < limit and len(rows) % 16 == 0:
            break
        if rest[row, column] == 0.0:
            columns.append(np.zeros_like(rest[:, 0]))
            rows.append(np.zeros_like(rest[0]))
            continue
        columns.append(rest[:, column] / rest[row, column])
        rows.append(rest[row].copy())
        rest = rest - np.outer(columns[-1], rows[-1])
    return np.stack(columns, axis=1), np.stack(rows, axis=0)


def halves(value):
    high = value.astype(jnp.bfloat16)
    return high, (value - high.astype(jnp.float32)).astype(jnp.bfloat16)


def dot(left, right):
    return jnp.dot(left, right, preferred_element_type=jnp.float32)


def kernel(
    sizes, in_ref, cols_ref, weight_ref, mx_ref, my_ref, spread_ref, out_ref,
    vel, ret, fin, vhalo, shalo, gx, gy, tend, sx, sy, sz, gsend, grecv, psend, precv,
    send_sem, recv_sem,
):
    n_gz, n_xy, width, scale = sizes
    _, rows_all, cols_all = in_ref.shape
    half = cols_all // 2
    chunk = rows_all // CHUNKS
    step = min(ROWS, chunk)
    grp, gz, xy = lax.axis_index("grp"), lax.axis_index("gz"), lax.axis_index("xy")
    domain = lax.rem(gz, 2)
    pair = gz - domain
    level = pair + grp
    levels = n_gz
    swapped = domain != grp
    has_up = level < levels - 1
    has_down = level > 0
    is_farm = domain == 0

    def at_level(other):
        other = lax.rem(other + levels, levels)
        parity = lax.rem(other, 2)
        return (parity, other - parity + domain, xy)

    up, down = at_level(level + 1), at_level(level - 1)
    swap_to = (domain, pair + grp, xy)
    mid_to = (grp, pair + 1 - domain, xy)
    end_to = (1 - grp, gz, xy)

    def xy_to(offset):
        return (grp, gz, lax.rem(xy + offset, n_xy))

    slots = {}

    def copy(name, source, target, device):
        slot = slots.setdefault(name, len(slots))
        return pltpu.make_async_remote_copy(
            src_ref=source, dst_ref=target, send_sem=send_sem.at[slot],
            recv_sem=recv_sem.at[slot], device_id=device, device_id_type=MESH,
        )

    chunks = list(range(CHUNKS))

    def region(ref, k):
        return ref.at[:, pl.ds(k * chunk, chunk), :]

    def flush(condition, copies):
        def wait():
            for item in copies:
                item.wait_send()

        if condition is None:
            wait()
        else:
            pl.when(condition)(wait)

    barrier = pltpu.get_barrier_semaphore()
    for device in [up, down, mid_to, end_to] + [xy_to(o) for o in range(1, n_xy)]:
        pl.semaphore_signal(barrier, inc=1, device_id=device, device_id_type=MESH)

    @pl.when(swapped)
    def _():
        pl.semaphore_signal(barrier, inc=1, device_id=swap_to, device_id_type=MESH)
        pl.semaphore_wait(barrier, 4 + n_xy)

    @pl.when(jnp.logical_not(swapped))
    def _():
        pl.semaphore_wait(barrier, 3 + n_xy)

    def z_copy(kind, s, k, upward):
        source, halo = (vel, vhalo) if kind == "v" else (sz, shalo)
        side, device = (0, up) if upward else (1, down)
        return copy((kind, s, side, k), region(source.at[s], k), region(halo.at[s, side], k), device)

    def z_start(kind, s, k):
        upward, downward = z_copy(kind, s, k, True), z_copy(kind, s, k, False)
        pl.when(jnp.logical_and(has_up, grp == 1))(upward.start)
        pl.when(has_down)(downward.start)
        pl.when(jnp.logical_and(has_up, grp == 0))(upward.start)

    def z_wait(kind, s, pieces):
        def wait(upward):
            for k in pieces:
                z_copy(kind, s, k, upward).wait_recv()

        pl.when(has_down)(lambda: wait(True))
        pl.when(has_up)(lambda: wait(False))

    def z_flush(kind, s):
        flush(has_up, [z_copy(kind, s, k, True) for k in chunks])
        flush(has_down, [z_copy(kind, s, k, False) for k in chunks])

    def swap_in(k):
        return copy(("in", k), region(in_ref, k), region(vel.at[0], k), swap_to)

    def swap_back(k):
        return copy(("out", k), region(ret, k), region(fin, k), swap_to)

    def fringe_copy(s, k):
        device = end_to if s == STEPS - 1 else mid_to
        return copy(("f", s, k), region(psend.at[s], k), region(precv.at[s], k), device)

    def g_copy(index, o, c):
        return copy(("g", index, o, c), gsend.at[index, c], grecv.at[index, o - 1, c], xy_to(o))

    @pl.when(swapped)
    def _():
        for k in chunks:
            swap_in(k).start()

    @pl.when(jnp.logical_not(swapped))
    def _():
        vel[0] = in_ref[...]

    @pl.when(level == 0)
    def _():
        for s in range(STEPS):
            vhalo[s, 0] = jnp.zeros_like(vel[0])
            shalo[s, 0] = jnp.zeros_like(vel[0])

    @pl.when(level == levels - 1)
    def _():
        for s in range(STEPS):
            vhalo[s, 1] = jnp.zeros_like(vel[0])
            shalo[s, 1] = jnp.zeros_like(vel[0])

    picker = jnp.where(
        lax.broadcasted_iota(jnp.int32, (cols_all, width), 0) == cols_ref[...], 1.0, 0.0
    ).astype(jnp.bfloat16)

    def picked(field):
        high = field.astype(jnp.bfloat16)
        rest = field - high.astype(jnp.float32)
        middle = rest.astype(jnp.bfloat16)
        low = (rest - middle.astype(jnp.float32)).astype(jnp.bfloat16)
        wide = dot(jnp.concatenate([high, middle, low], axis=0), picker)
        lines = field.shape[0]
        return (wide[:lines] + (wide[lines : 2 * lines] + wide[2 * lines :])) * weight_ref[...]

    def x_derived(field):
        left, right = field[:, :half], field[:, half:]
        both = []
        for at, value in ((0, left + right), (2, left - right)):
            high, low = halves(value)
            wide = dot(jnp.concatenate([high, low], axis=0), mx_ref[at])
            both.append(wide[:rows_all] + (wide[rows_all:] + dot(high, mx_ref[at + 1])))
        return jnp.concatenate([both[0] + both[1], both[0] - both[1]], axis=1)

    def y_derived(index, c, field):
        high, low = halves(field)
        lines = my_ref.shape[0] // 2
        wide = dot(my_ref[...], high)
        total = wide[:lines] + (wide[lines:] + dot(my_ref[:lines, :], low))
        gsend[index, c] = total[rows_all:]
        for o in range(1, n_xy):
            g_copy(index, o, c).start()
        return total[:rows_all]

    def received(index, c):
        result = None
        for o in range(1, n_xy):
            g_copy(index, o, c).wait_recv()
            high, low = halves(grecv[index, o - 1, c])
            term = dot(spread_ref[o - 1], jnp.concatenate([high, high, low], axis=0))
            result = term if result is None else result + term
        return result

    def g_flush(index):
        flush(None, [g_copy(index, o, c) for o in range(1, n_xy) for c in range(3)])

    def derive(s, c):
        field = vel[s, c]
        gy[c] = y_derived(2 * s, c, field)
        gx[c] = x_derived(field)

    z_scale = 1.0 / (2.0 * level_gap)

    for k in chunks:
        pl.when(swapped)(swap_in(k).wait_recv)
        z_start("v", 0, k)

    for s in range(STEPS):
        last = s == STEPS - 1
        for c in range(3):
            derive(s, c)
        if n_xy > 1:
            for c in range(3):
                gy[c] = gy[c] + received(2 * s, c)

        def pointwise(i, carry):
            for first in range(0, cols_all, BLOCK):
                block(pl.ds(pl.multiple_of(i * step, step), step), pl.ds(first, BLOCK))
            return carry

        def block(rows, lanes):
            u = [vel[s, c, rows, lanes] for c in range(3)]
            dx = [gx[c, rows, lanes] for c in range(3)]
            dy = [gy[c, rows, lanes] for c in range(3)]
            dz = [(vhalo[s, 1, c, rows, lanes] - vhalo[s, 0, c, rows, lanes]) * z_scale for c in range(3)]
            for c in range(3):
                tend[c, rows, lanes] = -(u[0] * dx[c] + u[1] * dy[c] + u[2] * dz[c])
            xx, yy, zz = dx[0], dy[1], dz[2]
            xy_, xz, yz = 0.5 * (dy[0] + dx[1]), 0.5 * (dz[0] + dx[2]), 0.5 * (dz[1] + dy[2])
            total = xx * xx + yy * yy + zz * zz + 2.0 * (xy_ * xy_ + xz * xz + yz * yz)
            eddy = (2.0 * scale) * jnp.sqrt(2.0 * total)
            xy_, xz, yz = eddy * xy_, eddy * xz, eddy * yz
            sx[0, rows, lanes] = eddy * xx
            sx[1, rows, lanes] = xy_
            sx[2, rows, lanes] = xz
            sy[0, rows, lanes] = xy_
            sy[1, rows, lanes] = eddy * yy
            sy[2, rows, lanes] = yz
            sz[s, 0, rows, lanes] = xz
            sz[s, 1, rows, lanes] = yz
            sz[s, 2, rows, lanes] = eddy * zz

        for k in chunks:
            z_wait("v", s, [k])
            lax.fori_loop(k * chunk // step, (k + 1) * chunk // step, pointwise, 0)
            z_start("s", s, k)

        for c in range(3):
            tend[c] = tend[c] + y_derived(2 * s + 1, c, sy[c])
            tend[c] = tend[c] + x_derived(sx[c])
        if n_xy > 1:
            for c in range(3):
                tend[c] = tend[c] + received(2 * s + 1, c)
        z_flush("v", s)
        g_flush(2 * s)
        g_flush(2 * s + 1)

        def update(k, target):
            rows = pl.ds(k * chunk, chunk)
            for c in range(3):
                along_z = (shalo[s, 1, c, rows, :] - shalo[s, 0, c, rows, :]) * z_scale
                target[c, rows, :] = vel[s, c, rows, :] + time_step * (tend[c, rows, :] + along_z)

        def pick(k, source):
            rows = pl.ds(k * chunk, chunk)
            fields = jnp.concatenate([source[c, rows, :] for c in range(3)], axis=0)
            values = picked(fields)
            for c in range(3):
                psend[s, c, rows, :] = values[c * chunk : (c + 1) * chunk]
            fringe_copy(s, k).start()

        def blend(k, source, target):
            fringe_copy(s, k).wait_recv()
            rows = pl.ds(k * chunk, chunk)
            for c in range(3):
                own = source[c, rows, :width] * (1.0 - weight_ref[...])
                target[c, rows, :width] = own + precv[s, c, rows, :]

        if not last:
            following = vel.at[s + 1]
            for k in chunks:
                z_wait("s", s, [k])
                update(k, following)

                @pl.when(jnp.logical_not(is_farm))
                def _():
                    pick(k, following)

                pl.when(is_farm)(lambda: blend(k, following, following))
                z_start("v", s + 1, k)
            z_flush("s", s)
            flush(jnp.logical_not(is_farm), [fringe_copy(s, k) for k in chunks])
        else:
            def finish(k):
                pl.when(swapped)(swap_back(k).wait_recv)
                pl.when(grp == 1)(lambda: pick(k, fin))
                rows = pl.ds(k * chunk, chunk)
                out_ref[:, rows, :] = fin[:, rows, :]
                pl.when(grp == 0)(lambda: blend(k, fin, out_ref))

            for k in chunks:
                z_wait("s", s, [k])

                @pl.when(swapped)
                def _():
                    update(k, ret)
                    swap_back(k).start()

                pl.when(jnp.logical_not(swapped))(lambda: update(k, fin))
                if k == 1:
                    flush(swapped, [swap_in(piece) for piece in chunks])
                if k > 0:
                    finish(k - 1)
            finish(CHUNKS - 1)
            z_flush("s", s)
            flush(swapped, [swap_back(k) for k in chunks])
            flush(grp == 1, [fringe_copy(s, k) for k in chunks])


def per_device(velocity, fringe_columns):
    _, comps, _, rows_all, cols_all = velocity.shape
    n_xy, n_gz = lax.axis_size("xy"), lax.axis_size("gz")
    cross = rows_all * n_xy
    delta = (2.0 * math.pi / cols_all * (2.0 * math.pi / cross) * level_gap) ** (1.0 / 3.0)
    width = fringe_columns.shape[0]
    half = cols_all // 2
    along = derivative_matrix(cols_all).T
    same, other = along[:half, :half], along[half:, :half]
    mx = np.concatenate([two_parts((same + other) / 2), two_parts((same - other) / 2)])
    across = derivative_matrix(cross)
    if n_xy > 1:
        spread, gather = factored(across[rows_all:, :rows_all])
    else:
        spread, gather = np.zeros((rows_all, 16)), np.zeros((16, rows_all))
    rank = gather.shape[0]
    my = np.concatenate(two_parts(np.concatenate([across[:rows_all, :rows_all], gather])))
    high, low = two_parts(spread)
    spread = np.concatenate([high, low, high], axis=1).reshape(-1, rows_all, 3 * rank)
    others = spread.shape[0]
    offsets = np.arange(width)
    weights = (0.5 * (1.0 + np.cos(np.pi * offsets / width))).astype(np.float32)[None]
    plane = (comps, rows_all, cols_all)
    fringe = (comps, rows_all, width)
    copies = STEPS * (5 * CHUNKS + 6 * others) + 2 * CHUNKS
    vmem = pl.BlockSpec(memory_space=pltpu.VMEM)

    def buffer(*shape):
        return pltpu.VMEM(shape, jnp.float32)

    result = pl.pallas_call(
        functools.partial(kernel, (n_gz, n_xy, width, (smag_coeff * delta) ** 2)),
        out_shape=jax.ShapeDtypeStruct(plane, jnp.float32),
        in_specs=[vmem] * 6,
        out_specs=vmem,
        scratch_shapes=[
            buffer(STEPS, *plane),
            buffer(*plane),
            buffer(*plane),
            buffer(STEPS, 2, *plane),
            buffer(STEPS, 2, *plane),
            buffer(*plane),
            buffer(*plane),
            buffer(*plane),
            buffer(*plane),
            buffer(*plane),
            buffer(STEPS, *plane),
            buffer(2 * STEPS, comps, rank, cols_all),
            buffer(2 * STEPS, others, comps, rank, cols_all),
            buffer(STEPS, *fringe),
            buffer(STEPS, *fringe),
            pltpu.SemaphoreType.DMA((copies,)),
            pltpu.SemaphoreType.DMA((copies,)),
        ],
        compiler_params=pltpu.CompilerParams(
            collective_id=0, has_side_effects=True, vmem_limit_bytes=56 * 1024 * 1024
        ),
    )(
        velocity.reshape(plane), fringe_columns.reshape(1, width), jnp.asarray(weights),
        jnp.asarray(mx), jnp.asarray(my), jnp.asarray(spread),
    )
    return result.reshape(velocity.shape)


def solution(mesh):
    in_specs = (P("grp", None, "gz", "xy", None), P())
    out_specs = P("grp", None, "gz", "xy", None)
    return jax.shard_map(
        per_device, mesh=mesh, in_specs=in_specs, out_specs=out_specs, check_vma=False
    )
```

```python
import functools
import math

import jax
import jax.numpy as jnp
import ml_dtypes
import numpy as np
from jax import lax
from jax.experimental import pallas as pl
from jax.experimental.pallas import tpu as pltpu
from jax.sharding import PartitionSpec as P

STEPS = 2
CHUNKS = 4
ROWS = 16
BLOCK = 128

time_step = 0.001
level_gap = 0.05
smag_coeff = 0.16
MESH = pl.DeviceIdType.MESH


def derivative_matrix(points):
    offsets = np.arange(points)
    distance = offsets[:, None] - offsets[None, :]
    safe = np.where(distance == 0, 1, distance)
    entries = 0.5 * (1.0 - 2.0 * (distance % 2)) / np.tan(np.pi * safe / points)
    return np.where(distance == 0, 0.0, entries)


def two_parts(matrix):
    single = matrix.astype(np.float32)
    high = single.astype(ml_dtypes.bfloat16)
    low = (single - high.astype(np.float32)).astype(ml_dtypes.bfloat16)
    return np.stack([high, low])


def factored(block):
    rest = block.copy()
    limit = np.abs(block).max() * 2.0**-30
    columns, rows = [], []
    while len(rows) < block.shape[1]:
        row, column = np.unravel_index(np.argmax(np.abs(rest)), rest.shape)
        if abs(rest[row, column]) < limit and len(rows) % 16 == 0:
            break
        if rest[row, column] == 0.0:
            columns.append(np.zeros_like(rest[:, 0]))
            rows.append(np.zeros_like(rest[0]))
            continue
        columns.append(rest[:, column] / rest[row, column])
        rows.append(rest[row].copy())
        rest = rest - np.outer(columns[-1], rows[-1])
    return np.stack(columns, axis=1), np.stack(rows, axis=0)


def halves(value):
    high = value.astype(jnp.bfloat16)
    return high, (value - high.astype(jnp.float32)).astype(jnp.bfloat16)


def dot(left, right):
    return jnp.dot(left, right, preferred_element_type=jnp.float32)


def kernel(
    sizes, in_ref, cols_ref, weight_ref, mx_ref, my_ref, spread_ref, out_ref,
    vel, ret, fin, vhalo, shalo, gx, gy, tend, sx, sy, sz, gsend, grecv, psend, precv,
    send_sem, recv_sem,
):
    n_gz, n_xy, width, scale = sizes
    _, rows_all, cols_all = in_ref.shape
    half = cols_all // 2
    chunk = rows_all // CHUNKS
    step = min(ROWS, chunk)
    grp, gz, xy = lax.axis_index("grp"), lax.axis_index("gz"), lax.axis_index("xy")
    domain = lax.rem(gz, 2)
    pair = gz - domain
    level = pair + grp
    levels = n_gz
    swapped = domain != grp
    has_up = level < levels - 1
    has_down = level > 0
    is_farm = domain == 0

    def at_level(other):
        other = lax.rem(other + levels, levels)
        parity = lax.rem(other, 2)
        return (parity, other - parity + domain, xy)

    up, down = at_level(level + 1), at_level(level - 1)
    swap_to = (domain, pair + grp, xy)
    mid_to = (grp, pair + 1 - domain, xy)
    end_to = (1 - grp, gz, xy)
    farm_to = (0, pair + grp, xy)

    def xy_to(offset):
        return (grp, gz, lax.rem(xy + offset, n_xy))

    slots = {}

    def copy(name, source, target, device):
        slot = slots.setdefault(name, len(slots))
        return pltpu.make_async_remote_copy(
            src_ref=source, dst_ref=target, send_sem=send_sem.at[slot],
            recv_sem=recv_sem.at[slot], device_id=device, device_id_type=MESH,
        )

    chunks = list(range(CHUNKS))

    def region(ref, k, lanes=None):
        first, count = lanes or (0, ref.shape[-1])
        return ref.at[:, pl.ds(k * chunk, chunk), pl.ds(first, count)]

    def spans(kind, s):
        if kind == "v" and s > 0:
            return [(width, cols_all - width), (0, width)]
        return [(0, cols_all)]

    def flush(condition, copies):
        def wait():
            for item in copies:
                item.wait_send()

        if condition is None:
            wait()
        else:
            pl.when(condition)(wait)

    barrier = pltpu.get_barrier_semaphore()
    for device in [up, down, mid_to, end_to] + [xy_to(o) for o in range(1, n_xy)]:
        pl.semaphore_signal(barrier, inc=1, device_id=device, device_id_type=MESH)

    @pl.when(swapped)
    def _():
        pl.semaphore_signal(barrier, inc=1, device_id=swap_to, device_id_type=MESH)
        pl.semaphore_wait(barrier, 4 + n_xy)

    @pl.when(jnp.logical_not(swapped))
    def _():
        pl.semaphore_wait(barrier, 3 + n_xy)

    def z_copy(kind, s, k, upward, lanes):
        source, halo = (vel, vhalo) if kind == "v" else (sz, shalo)
        side, device = (0, up) if upward else (1, down)
        return copy(
            (kind, s, side, k, lanes),
            region(source.at[s], k, lanes), region(halo.at[s, side], k, lanes), device,
        )

    def z_start(kind, s, k, lanes=None):
        lanes = lanes or (0, cols_all)
        upward, downward = z_copy(kind, s, k, True, lanes), z_copy(kind, s, k, False, lanes)
        pl.when(jnp.logical_and(has_up, grp == 1))(upward.start)
        pl.when(has_down)(downward.start)
        pl.when(jnp.logical_and(has_up, grp == 0))(upward.start)

    def z_wait(kind, s, k):
        def wait(upward):
            for lanes in spans(kind, s):
                z_copy(kind, s, k, upward, lanes).wait_recv()

        pl.when(has_down)(lambda: wait(True))
        pl.when(has_up)(lambda: wait(False))

    def z_flush(kind, s):
        for condition, upward in ((has_up, True), (has_down, False)):
            flush(condition, [z_copy(kind, s, k, upward, lanes) for k in chunks for lanes in spans(kind, s)])

    def swap_in(k):
        return copy(("in", k), region(in_ref, k), region(vel.at[0], k), swap_to)

    def swap_back(k):
        return copy(("out", k), region(ret, k), region(fin, k), swap_to)

    def fringe_copy(s, k):
        device = farm_to if s == STEPS - 1 else mid_to
        return copy(("f", s, k), region(psend.at[s], k), region(precv.at[s], k), device)

    def g_copy(index, o, c):
        return copy(("g", index, o, c), gsend.at[index, c], grecv.at[index, o - 1, c], xy_to(o))

    @pl.when(swapped)
    def _():
        for k in chunks:
            swap_in(k).start()

    @pl.when(jnp.logical_not(swapped))
    def _():
        vel[0] = in_ref[...]

    @pl.when(level == 0)
    def _():
        for s in range(STEPS):
            vhalo[s, 0] = jnp.zeros_like(vel[0])
            shalo[s, 0] = jnp.zeros_like(vel[0])

    @pl.when(level == levels - 1)
    def _():
        for s in range(STEPS):
            vhalo[s, 1] = jnp.zeros_like(vel[0])
            shalo[s, 1] = jnp.zeros_like(vel[0])

    picker = jnp.where(
        lax.broadcasted_iota(jnp.int32, (cols_all, width), 0) == cols_ref[...], 1.0, 0.0
    ).astype(jnp.bfloat16)

    def picked(field):
        high = field.astype(jnp.bfloat16)
        rest = field - high.astype(jnp.float32)
        middle = rest.astype(jnp.bfloat16)
        low = (rest - middle.astype(jnp.float32)).astype(jnp.bfloat16)
        wide = dot(jnp.concatenate([high, middle, low], axis=0), picker)
        lines = field.shape[0]
        return (wide[:lines] + (wide[lines : 2 * lines] + wide[2 * lines :])) * weight_ref[...]

    def x_derived(field):
        left, right = field[:, :half], field[:, half:]
        both = []
        for at, value in ((0, left + right), (2, left - right)):
            high, low = halves(value)
            wide = dot(jnp.concatenate([high, low], axis=0), mx_ref[at])
            both.append(wide[:rows_all] + (wide[rows_all:] + dot(high, mx_ref[at + 1])))
        return jnp.concatenate([both[0] + both[1], both[0] - both[1]], axis=1)

    def y_derived(index, c, field):
        high, low = halves(field)
        lines = my_ref.shape[0] // 2
        wide = dot(my_ref[...], high)
        total = wide[:lines] + (wide[lines:] + dot(my_ref[:lines, :], low))
        gsend[index, c] = total[rows_all:]
        for o in range(1, n_xy):
            g_copy(index, o, c).start()
        return total[:rows_all]

    def received(index, c):
        result = None
        for o in range(1, n_xy):
            g_copy(index, o, c).wait_recv()
            high, low = halves(grecv[index, o - 1, c])
            term = dot(spread_ref[o - 1], jnp.concatenate([high, high, low], axis=0))
            result = term if result is None else result + term
        return result

    def g_flush(index):
        flush(None, [g_copy(index, o, c) for o in range(1, n_xy) for c in range(3)])

    def derive(s, c):
        field = vel[s, c]
        gy[c] = y_derived(2 * s, c, field)
        gx[c] = x_derived(field)

    z_scale = 1.0 / (2.0 * level_gap)

    for k in chunks:
        pl.when(swapped)(swap_in(k).wait_recv)
        z_start("v", 0, k)

    for s in range(STEPS):
        last = s == STEPS - 1
        for c in range(3):
            derive(s, c)
        if n_xy > 1:
            for c in range(3):
                gy[c] = gy[c] + received(2 * s, c)

        def pointwise(i, carry):
            for first in range(0, cols_all, BLOCK):
                block(pl.ds(pl.multiple_of(i * step, step), step), pl.ds(first, BLOCK))
            return carry

        def block(rows, lanes):
            u = [vel[s, c, rows, lanes] for c in range(3)]
            dx = [gx[c, rows, lanes] for c in range(3)]
            dy = [gy[c, rows, lanes] for c in range(3)]
            dz = [(vhalo[s, 1, c, rows, lanes] - vhalo[s, 0, c, rows, lanes]) * z_scale for c in range(3)]
            for c in range(3):
                tend[c, rows, lanes] = -(u[0] * dx[c] + u[1] * dy[c] + u[2] * dz[c])
            xx, yy, zz = dx[0], dy[1], dz[2]
            xy_, xz, yz = 0.5 * (dy[0] + dx[1]), 0.5 * (dz[0] + dx[2]), 0.5 * (dz[1] + dy[2])
            total = xx * xx + yy * yy + zz * zz + 2.0 * (xy_ * xy_ + xz * xz + yz * yz)
            eddy = (2.0 * scale) * jnp.sqrt(2.0 * total)
            xy_, xz, yz = eddy * xy_, eddy * xz, eddy * yz
            sx[0, rows, lanes] = eddy * xx
            sx[1, rows, lanes] = xy_
            sx[2, rows, lanes] = xz
            sy[0, rows, lanes] = xy_
            sy[1, rows, lanes] = eddy * yy
            sy[2, rows, lanes] = yz
            sz[s, 0, rows, lanes] = xz
            sz[s, 1, rows, lanes] = yz
            sz[s, 2, rows, lanes] = eddy * zz

        for k in chunks:
            z_wait("v", s, k)
            lax.fori_loop(k * chunk // step, (k + 1) * chunk // step, pointwise, 0)
            z_start("s", s, k)

        for c in range(3):
            tend[c] = tend[c] + y_derived(2 * s + 1, c, sy[c])
            tend[c] = tend[c] + x_derived(sx[c])
        if n_xy > 1:
            for c in range(3):
                tend[c] = tend[c] + received(2 * s + 1, c)
        z_flush("v", s)
        g_flush(2 * s)
        g_flush(2 * s + 1)

        def update(k, target):
            rows = pl.ds(k * chunk, chunk)
            for c in range(3):
                along_z = (shalo[s, 1, c, rows, :] - shalo[s, 0, c, rows, :]) * z_scale
                target[c, rows, :] = vel[s, c, rows, :] + time_step * (tend[c, rows, :] + along_z)

        def pick(k, source):
            rows = pl.ds(k * chunk, chunk)
            fields = jnp.concatenate([source[c, rows, :] for c in range(3)], axis=0)
            values = picked(fields)
            for c in range(3):
                psend[s, c, rows, :] = values[c * chunk : (c + 1) * chunk]
            fringe_copy(s, k).start()

        def blend(k, source, target):
            fringe_copy(s, k).wait_recv()
            rows = pl.ds(k * chunk, chunk)
            for c in range(3):
                own = source[c, rows, :width] * (1.0 - weight_ref[...])
                target[c, rows, :width] = own + precv[s, c, rows, :]

        if not last:
            following = vel.at[s + 1]
            beyond, within = spans("v", s + 1)
            for k in chunks:
                z_wait("s", s, k)
                update(k, following)
                z_start("v", s + 1, k, beyond)

                @pl.when(jnp.logical_not(is_farm))
                def _():
                    pick(k, following)
                    z_start("v", s + 1, k, within)

            @pl.when(is_farm)
            def _():
                for k in chunks:
                    blend(k, following, following)
                    z_start("v", s + 1, k, within)

            z_flush("s", s)
            flush(jnp.logical_not(is_farm), [fringe_copy(s, k) for k in chunks])
        else:
            def finish(k):
                pl.when(swapped)(swap_back(k).wait_recv)
                rows = pl.ds(k * chunk, chunk)
                out_ref[:, rows, :] = fin[:, rows, :]
                pl.when(grp == 0)(lambda: blend(k, fin, out_ref))

            def advance(k, target):
                update(k, target)
                if target is ret:
                    swap_back(k).start()
                pl.when(jnp.logical_not(is_farm))(lambda: pick(k, target))

            for k in chunks:
                z_wait("s", s, k)
                pl.when(swapped)(lambda: advance(k, ret))
                pl.when(jnp.logical_not(swapped))(lambda: advance(k, fin))
                if k > 1:
                    finish(k - 2)
            for k in chunks[-2:]:
                finish(k)
            flush(swapped, [swap_in(k) for k in chunks])
            z_flush("s", s)
            flush(swapped, [swap_back(k) for k in chunks])
            flush(jnp.logical_not(is_farm), [fringe_copy(s, k) for k in chunks])


def per_device(velocity, fringe_columns):
    _, comps, _, rows_all, cols_all = velocity.shape
    n_xy, n_gz = lax.axis_size("xy"), lax.axis_size("gz")
    cross = rows_all * n_xy
    delta = (2.0 * math.pi / cols_all * (2.0 * math.pi / cross) * level_gap) ** (1.0 / 3.0)
    width = fringe_columns.shape[0]
    half = cols_all // 2
    along = derivative_matrix(cols_all).T
    same, other = along[:half, :half], along[half:, :half]
    mx = np.concatenate([two_parts((same + other) / 2), two_parts((same - other) / 2)])
    across = derivative_matrix(cross)
    if n_xy > 1:
        spread, gather = factored(across[rows_all:, :rows_all])
    else:
        spread, gather = np.zeros((rows_all, 16)), np.zeros((16, rows_all))
    rank = gather.shape[0]
    my = np.concatenate(two_parts(np.concatenate([across[:rows_all, :rows_all], gather])))
    high, low = two_parts(spread)
    spread = np.concatenate([high, low, high], axis=1).reshape(-1, rows_all, 3 * rank)
    others = spread.shape[0]
    offsets = np.arange(width)
    weights = (0.5 * (1.0 + np.cos(np.pi * offsets / width))).astype(np.float32)[None]
    plane = (comps, rows_all, cols_all)
    fringe = (comps, rows_all, width)
    copies = STEPS * (7 * CHUNKS + 6 * others) + 2 * CHUNKS
    vmem = pl.BlockSpec(memory_space=pltpu.VMEM)

    def buffer(*shape):
        return pltpu.VMEM(shape, jnp.float32)

    result = pl.pallas_call(
        functools.partial(kernel, (n_gz, n_xy, width, (smag_coeff * delta) ** 2)),
        out_shape=jax.ShapeDtypeStruct(plane, jnp.float32),
        in_specs=[vmem] * 6,
        out_specs=vmem,
        scratch_shapes=[
            buffer(STEPS, *plane),
            buffer(*plane),
            buffer(*plane),
            buffer(STEPS, 2, *plane),
            buffer(STEPS, 2, *plane),
            buffer(*plane),
            buffer(*plane),
            buffer(*plane),
            buffer(*plane),
            buffer(*plane),
            buffer(STEPS, *plane),
            buffer(2 * STEPS, comps, rank, cols_all),
            buffer(2 * STEPS, others, comps, rank, cols_all),
            buffer(STEPS, *fringe),
            buffer(STEPS, *fringe),
            pltpu.SemaphoreType.DMA((copies,)),
            pltpu.SemaphoreType.DMA((copies,)),
        ],
        compiler_params=pltpu.CompilerParams(
            collective_id=0, has_side_effects=True, vmem_limit_bytes=56 * 1024 * 1024
        ),
    )(
        velocity.reshape(plane), fringe_columns.reshape(1, width), jnp.asarray(weights),
        jnp.asarray(mx), jnp.asarray(my), jnp.asarray(spread),
    )
    return result.reshape(velocity.shape)


def solution(mesh):
    in_specs = (P("grp", None, "gz", "xy", None), P())
    out_specs = P("grp", None, "gz", "xy", None)
    return jax.shard_map(
        per_device, mesh=mesh, in_specs=in_specs, out_specs=out_specs, check_vma=False
    )
```

```python
import functools
import math

import jax
import jax.numpy as jnp
import ml_dtypes
import numpy as np
from jax import lax
from jax.experimental import pallas as pl
from jax.experimental.pallas import tpu as pltpu
from jax.sharding import PartitionSpec as P

STEPS = 2
CHUNKS = 4
ROWS = 8

time_step = 0.001
level_gap = 0.05
smag_coeff = 0.16
MESH = pl.DeviceIdType.MESH


def derivative_matrix(points):
    offsets = np.arange(points)
    distance = offsets[:, None] - offsets[None, :]
    safe = np.where(distance == 0, 1, distance)
    entries = 0.5 * (1.0 - 2.0 * (distance % 2)) / np.tan(np.pi * safe / points)
    return np.where(distance == 0, 0.0, entries)


def two_parts(matrix):
    single = matrix.astype(np.float32)
    high = single.astype(ml_dtypes.bfloat16)
    low = (single - high.astype(np.float32)).astype(ml_dtypes.bfloat16)
    return np.stack([high, low])


def factored(block):
    rest = block.copy()
    limit = np.abs(block).max() * 2.0**-30
    columns, rows = [], []
    while len(rows) < block.shape[1]:
        row, column = np.unravel_index(np.argmax(np.abs(rest)), rest.shape)
        if abs(rest[row, column]) < limit and len(rows) % 16 == 0:
            break
        if rest[row, column] == 0.0:
            columns.append(np.zeros_like(rest[:, 0]))
            rows.append(np.zeros_like(rest[0]))
            continue
        columns.append(rest[:, column] / rest[row, column])
        rows.append(rest[row].copy())
        rest = rest - np.outer(columns[-1], rows[-1])
    return np.stack(columns, axis=1), np.stack(rows, axis=0)


def halves(value):
    high = value.astype(jnp.bfloat16)
    return high, (value - high.astype(jnp.float32)).astype(jnp.bfloat16)


def dot(left, right):
    return jnp.dot(left, right, preferred_element_type=jnp.float32)


def dot_parts(left, right):
    return dot(left[0], right[0]) + (dot(left[0], right[1]) + dot(left[1], right[0]))


def kernel(
    sizes, in_ref, cols_ref, weight_ref, mx_ref, my_ref, gather_ref, spread_ref, out_ref, picks_ref,
    vel, ret, fin, vhalo, shalo, gx, gy, tend, sx, sy, sz, gsend, grecv, psend, precv,
    send_sem, recv_sem,
):
    n_gz, n_xy, width, scale = sizes
    _, rows_all, cols_all = in_ref.shape
    half = cols_all // 2
    chunk = rows_all // CHUNKS
    grp, gz, xy = lax.axis_index("grp"), lax.axis_index("gz"), lax.axis_index("xy")
    domain = lax.rem(gz, 2)
    pair = gz - domain
    level = pair + grp
    levels = n_gz
    swapped = domain != grp
    has_up = level < levels - 1
    has_down = level > 0
    is_farm = domain == 0

    def at_level(other):
        other = lax.rem(other + levels, levels)
        parity = lax.rem(other, 2)
        return (parity, other - parity + domain, xy)

    up, down = at_level(level + 1), at_level(level - 1)
    swap_to = (domain, pair + grp, xy)
    mid_to = (grp, pair + 1 - domain, xy)
    end_to = (1 - grp, gz, xy)

    def xy_to(offset):
        return (grp, gz, lax.rem(xy + offset, n_xy))

    slots = {}

    def copy(name, source, target, device):
        slot = slots.setdefault(name, len(slots))
        return pltpu.make_async_remote_copy(
            src_ref=source, dst_ref=target, send_sem=send_sem.at[slot],
            recv_sem=recv_sem.at[slot], device_id=device, device_id_type=MESH,
        )

    pending = []

    def start(condition, item):
        pending.append((condition, item))
        if condition is None:
            item.start()
        else:
            pl.when(condition)(item.start)

    def part(ref, k):
        return ref.at[:, pl.ds(k * chunk, chunk), :]

    barrier = pltpu.get_barrier_semaphore()
    for device in [up, down, mid_to, end_to] + [xy_to(o) for o in range(1, n_xy)]:
        pl.semaphore_signal(barrier, inc=1, device_id=device, device_id_type=MESH)

    @pl.when(swapped)
    def _():
        pl.semaphore_signal(barrier, inc=1, device_id=swap_to, device_id_type=MESH)
        pl.semaphore_wait(barrier, 4 + n_xy)

    @pl.when(jnp.logical_not(swapped))
    def _():
        pl.semaphore_wait(barrier, 3 + n_xy)

    def z_copies(kind, s, k):
        source, halo = (vel, vhalo) if kind == "v" else (sz, shalo)
        return (
            copy((kind, s, 0, k), part(source.at[s], k), part(halo.at[s, 0], k), up),
            copy((kind, s, 1, k), part(source.at[s], k), part(halo.at[s, 1], k), down),
        )

    def z_start(kind, s, k):
        upward, downward = z_copies(kind, s, k)
        start(has_up, upward)
        start(has_down, downward)

    def z_wait(kind, s, k):
        upward, downward = z_copies(kind, s, k)
        pl.when(has_down)(upward.wait_recv)
        pl.when(has_up)(downward.wait_recv)

    swap_in = [copy(("in", k), part(in_ref, k), part(vel.at[0], k), swap_to) for k in range(CHUNKS)]
    for k in range(CHUNKS):
        start(swapped, swap_in[k])

    @pl.when(jnp.logical_not(swapped))
    def _():
        vel[0] = in_ref[...]

    @pl.when(level == 0)
    def _():
        for s in range(STEPS):
            vhalo[s, 0] = jnp.zeros_like(vel[0])
            shalo[s, 0] = jnp.zeros_like(vel[0])

    @pl.when(level == levels - 1)
    def _():
        for s in range(STEPS):
            vhalo[s, 1] = jnp.zeros_like(vel[0])
            shalo[s, 1] = jnp.zeros_like(vel[0])

    for k in range(CHUNKS):
        pl.when(swapped)(swap_in[k].wait_recv)
        z_start("v", 0, k)

    picker = jnp.where(
        lax.broadcasted_iota(jnp.int32, (cols_all, width), 0) == cols_ref[...], 1.0, 0.0
    ).astype(jnp.bfloat16)

    def picked(field):
        high = field.astype(jnp.bfloat16)
        rest = field - high.astype(jnp.float32)
        middle = rest.astype(jnp.bfloat16)
        low = (rest - middle.astype(jnp.float32)).astype(jnp.bfloat16)
        return (dot(high, picker) + (dot(middle, picker) + dot(low, picker))) * weight_ref[...]

    def x_derived(field):
        left, right = field[:, :half], field[:, half:]
        total = dot_parts(halves(left + right), (mx_ref[0], mx_ref[1]))
        difference = dot_parts(halves(left - right), (mx_ref[2], mx_ref[3]))
        return jnp.concatenate([total + difference, total - difference], axis=1)

    def compress(index, read):
        def body(c, carry):
            gsend[index, c] = dot_parts((gather_ref[0], gather_ref[1]), halves(read(c)))
            return carry

        lax.fori_loop(0, 3, body, 0)
        for o in range(1, n_xy):
            start(None, compressed(index, o))

    def compressed(index, o):
        return copy(("g", index, o), gsend.at[index], grecv.at[index, o - 1], xy_to(o))

    def received(index, c):
        result = None
        for o in range(1, n_xy):
            term = dot_parts((spread_ref[0, o - 1], spread_ref[1, o - 1]), halves(grecv[index, o - 1, c]))
            result = term if result is None else result + term
        return result

    def g_wait(index):
        for o in range(1, n_xy):
            compressed(index, o).wait_recv()

    z_scale = 1.0 / (2.0 * level_gap)

    for s in range(STEPS):
        compress(2 * s, lambda c: vel[s, c])

        def first(c, carry):
            field = vel[s, c]
            gx[c] = x_derived(field)
            gy[c] = dot_parts((my_ref[0], my_ref[1]), halves(field))
            return carry

        lax.fori_loop(0, 3, first, 0)
        g_wait(2 * s)

        def second(c, carry):
            gy[c] = gy[c] + received(2 * s, c)
            return carry

        if n_xy > 1:
            lax.fori_loop(0, 3, second, 0)

        def pointwise(i, carry):
            rows = pl.ds(pl.multiple_of(i * ROWS, ROWS), ROWS)
            u = [vel[s, c, rows, :] for c in range(3)]
            dx = [gx[c, rows, :] for c in range(3)]
            dy = [gy[c, rows, :] for c in range(3)]
            dz = [(vhalo[s, 1, c, rows, :] - vhalo[s, 0, c, rows, :]) * z_scale for c in range(3)]
            for c in range(3):
                tend[c, rows, :] = -(u[0] * dx[c] + u[1] * dy[c] + u[2] * dz[c])
            xx, yy, zz = dx[0], dy[1], dz[2]
            xy_, xz, yz = 0.5 * (dy[0] + dx[1]), 0.5 * (dz[0] + dx[2]), 0.5 * (dz[1] + dy[2])
            total = xx * xx + yy * yy + zz * zz + 2.0 * (xy_ * xy_ + xz * xz + yz * yz)
            eddy = (2.0 * scale) * jnp.sqrt(2.0 * total)
            xy_, xz, yz = eddy * xy_, eddy * xz, eddy * yz
            sx[0, rows, :] = eddy * xx
            sx[1, rows, :] = xy_
            sx[2, rows, :] = xz
            sy[0, rows, :] = xy_
            sy[1, rows, :] = eddy * yy
            sy[2, rows, :] = yz
            sz[s, 0, rows, :] = xz
            sz[s, 1, rows, :] = yz
            sz[s, 2, rows, :] = eddy * zz
            return carry

        for k in range(CHUNKS):
            z_wait("v", s, k)
            lax.fori_loop(k * chunk // ROWS, (k + 1) * chunk // ROWS, pointwise, 0)
            z_start("s", s, k)

        compress(2 * s + 1, lambda c: sy[c])

        def third(c, carry):
            local = dot_parts((my_ref[0], my_ref[1]), halves(sy[c]))
            tend[c] = tend[c] + x_derived(sx[c]) + local
            return carry

        lax.fori_loop(0, 3, third, 0)
        g_wait(2 * s + 1)

        def fourth(c, carry):
            tend[c] = tend[c] + received(2 * s + 1, c)
            return carry

        if n_xy > 1:
            lax.fori_loop(0, 3, fourth, 0)

        last = s == STEPS - 1

        def updated(k, target):
            def body(i, carry):
                rows = pl.ds(pl.multiple_of(i * ROWS, ROWS), ROWS)
                for c in range(3):
                    along_z = (shalo[s, 1, c, rows, :] - shalo[s, 0, c, rows, :]) * z_scale
                    target[c, rows, :] = vel[s, c, rows, :] + time_step * (tend[c, rows, :] + along_z)
                return carry

            lax.fori_loop(k * chunk // ROWS, (k + 1) * chunk // ROWS, body, 0)

        def pick(k, source):
            rows = pl.ds(k * chunk, chunk)
            for c in range(3):
                psend[s, c, rows, :] = picked(source[c, rows, :])

        def blend(k, source, target):
            rows = pl.ds(k * chunk, chunk)
            for c in range(3):
                own = source[c, rows, :width] * (1.0 - weight_ref[...])
                target[c, rows, :width] = own + precv[s, c, rows, :]

        def fringe_copy(k, device):
            return copy(("f", s, k), part(psend.at[s], k), part(precv.at[s], k), device)

        if not last:
            following = vel.at[s + 1]
            for k in range(CHUNKS):
                z_wait("s", s, k)
                updated(k, following)

                @pl.when(jnp.logical_not(is_farm))
                def _():
                    pick(k, following)

                start(jnp.logical_not(is_farm), fringe_copy(k, mid_to))

                @pl.when(is_farm)
                def _():
                    fringe_copy(k, mid_to).wait_recv()
                    blend(k, following, following)

                z_start("v", s + 1, k)
        else:
            back = [copy(("out", k), part(ret, k), part(fin, k), swap_to) for k in range(CHUNKS)]
            for k in range(CHUNKS):
                z_wait("s", s, k)

                @pl.when(swapped)
                def _():
                    updated(k, ret)

                @pl.when(jnp.logical_not(swapped))
                def _():
                    updated(k, fin)

                start(swapped, back[k])
            for k in range(CHUNKS):
                pl.when(swapped)(back[k].wait_recv)

                @pl.when(grp == 1)
                def _():
                    pick(k, fin)

                start(grp == 1, fringe_copy(k, end_to))
                rows = pl.ds(k * chunk, chunk)
                out_ref[:, rows, :] = fin[:, rows, :]

                @pl.when(grp == 0)
                def _():
                    fringe_copy(k, end_to).wait_recv()
                    picks_ref[:, rows, :] = precv[s, :, rows, :]

                @pl.when(grp == 1)
                def _():
                    picks_ref[:, rows, :] = jnp.zeros((3, chunk, width), jnp.float32)

    for condition, item in pending:
        if condition is None:
            item.wait_send()
        else:
            pl.when(condition)(item.wait_send)


def per_device(velocity, fringe_columns):
    _, comps, _, rows_all, cols_all = velocity.shape
    n_xy, n_gz = lax.axis_size("xy"), lax.axis_size("gz")
    cross = rows_all * n_xy
    delta = (2.0 * math.pi / cols_all * (2.0 * math.pi / cross) * level_gap) ** (1.0 / 3.0)
    width = fringe_columns.shape[0]
    half = cols_all // 2
    along = derivative_matrix(cols_all).T
    same, other = along[:half, :half], along[half:, :half]
    mx = np.concatenate([two_parts((same + other) / 2), two_parts((same - other) / 2)])
    across = derivative_matrix(cross)
    my = two_parts(across[:rows_all, :rows_all])
    if n_xy > 1:
        spread, gather = factored(across[rows_all:, :rows_all])
    else:
        spread, gather = np.zeros((rows_all, 16)), np.zeros((16, rows_all))
    rank = gather.shape[0]
    gather = two_parts(gather)
    spread = two_parts(spread).reshape(2, -1, rows_all, rank)
    others = spread.shape[1]
    offsets = np.arange(width)
    weights = (0.5 * (1.0 + np.cos(np.pi * offsets / width))).astype(np.float32)[None]
    plane = (comps, rows_all, cols_all)
    fringe = (comps, rows_all, width)
    copies = STEPS * CHUNKS * 5 + 2 * CHUNKS + 2 * STEPS * others
    vmem = pl.BlockSpec(memory_space=pltpu.VMEM)

    def buffer(*shape):
        return pltpu.VMEM(shape, jnp.float32)

    result, picks = pl.pallas_call(
        functools.partial(kernel, (n_gz, n_xy, width, (smag_coeff * delta) ** 2)),
        out_shape=[jax.ShapeDtypeStruct(plane, jnp.float32), jax.ShapeDtypeStruct(fringe, jnp.float32)],
        in_specs=[vmem] * 7,
        out_specs=[vmem, vmem],
        scratch_shapes=[
            buffer(STEPS, *plane),
            buffer(*plane),
            buffer(*plane),
            buffer(STEPS, 2, *plane),
            buffer(STEPS, 2, *plane),
            buffer(*plane),
            buffer(*plane),
            buffer(*plane),
            buffer(*plane),
            buffer(*plane),
            buffer(STEPS, *plane),
            buffer(2 * STEPS, comps, rank, cols_all),
            buffer(2 * STEPS, others, comps, rank, cols_all),
            buffer(STEPS, *fringe),
            buffer(STEPS, *fringe),
            pltpu.SemaphoreType.DMA((copies,)),
            pltpu.SemaphoreType.DMA((copies,)),
        ],
        compiler_params=pltpu.CompilerParams(
            collective_id=0, has_side_effects=True, vmem_limit_bytes=56 * 1024 * 1024
        ),
    )(
        velocity.reshape(plane), fringe_columns.reshape(1, width), jnp.asarray(weights),
        jnp.asarray(mx), jnp.asarray(my), jnp.asarray(gather), jnp.asarray(spread),
    )
    kept = jnp.where(lax.axis_index("grp") == 0, 1.0 - jnp.asarray(weights), 1.0)
    kept = jnp.pad(kept, ((0, 0), (0, cols_all - width)), constant_values=1.0)
    added = jnp.pad(picks, ((0, 0), (0, 0), (0, cols_all - width)))
    return (result * kept + added).reshape(velocity.shape)


def solution(mesh):
    in_specs = (P("grp", None, "gz", "xy", None), P())
    out_specs = P("grp", None, "gz", "xy", None)
    return jax.shard_map(
        per_device, mesh=mesh, in_specs=in_specs, out_specs=out_specs, check_vma=False
    )
```

```python
import functools
import math

import jax
import jax.numpy as jnp
import ml_dtypes
import numpy as np
from jax import lax
from jax.experimental import pallas as pl
from jax.experimental.pallas import tpu as pltpu
from jax.sharding import PartitionSpec as P

STEPS = 2
CHUNKS = 4
ROWS = 8

time_step = 0.001
level_gap = 0.05
smag_coeff = 0.16
MESH = pl.DeviceIdType.MESH


def derivative_matrix(points):
    offsets = np.arange(points)
    distance = offsets[:, None] - offsets[None, :]
    safe = np.where(distance == 0, 1, distance)
    entries = 0.5 * (1.0 - 2.0 * (distance % 2)) / np.tan(np.pi * safe / points)
    return np.where(distance == 0, 0.0, entries)


def two_parts(matrix):
    single = matrix.astype(np.float32)
    high = single.astype(ml_dtypes.bfloat16)
    low = (single - high.astype(np.float32)).astype(ml_dtypes.bfloat16)
    return np.stack([high, low])


def factored(block):
    rest = block.copy()
    limit = np.abs(block).max() * 2.0**-30
    columns, rows = [], []
    while len(rows) < block.shape[1]:
        row, column = np.unravel_index(np.argmax(np.abs(rest)), rest.shape)
        if abs(rest[row, column]) < limit and len(rows) % 16 == 0:
            break
        if rest[row, column] == 0.0:
            columns.append(np.zeros_like(rest[:, 0]))
            rows.append(np.zeros_like(rest[0]))
            continue
        columns.append(rest[:, column] / rest[row, column])
        rows.append(rest[row].copy())
        rest = rest - np.outer(columns[-1], rows[-1])
    return np.stack(columns, axis=1), np.stack(rows, axis=0)


def halves(value):
    high = value.astype(jnp.bfloat16)
    return high, (value - high.astype(jnp.float32)).astype(jnp.bfloat16)


def dot(left, right):
    return jnp.dot(left, right, preferred_element_type=jnp.float32)


def dot_parts(left, right):
    return dot(left[0], right[0]) + (dot(left[0], right[1]) + dot(left[1], right[0]))


def kernel(
    sizes, in_ref, cols_ref, weight_ref, mx_ref, my_ref, gather_ref, spread_ref, out_ref,
    vel, ret, fin, vhalo, shalo, gx, gy, tend, sx, sy, sz, gsend, grecv, psend, precv,
    send_sem, recv_sem,
):
    n_gz, n_xy, width, scale = sizes
    _, rows_all, cols_all = in_ref.shape
    half = cols_all // 2
    chunk = rows_all // CHUNKS
    grp, gz, xy = lax.axis_index("grp"), lax.axis_index("gz"), lax.axis_index("xy")
    domain = lax.rem(gz, 2)
    pair = gz - domain
    level = pair + grp
    levels = n_gz
    swapped = domain != grp
    has_up = level < levels - 1
    has_down = level > 0
    is_farm = domain == 0

    def at_level(other):
        other = lax.rem(other + levels, levels)
        parity = lax.rem(other, 2)
        return (parity, other - parity + domain, xy)

    up, down = at_level(level + 1), at_level(level - 1)
    swap_to = (domain, pair + grp, xy)
    mid_to = (grp, pair + 1 - domain, xy)
    end_to = (1 - grp, gz, xy)

    def xy_to(offset):
        return (grp, gz, lax.rem(xy + offset, n_xy))

    slots = {}

    def copy(name, source, target, device):
        slot = slots.setdefault(name, len(slots))
        return pltpu.make_async_remote_copy(
            src_ref=source, dst_ref=target, send_sem=send_sem.at[slot],
            recv_sem=recv_sem.at[slot], device_id=device, device_id_type=MESH,
        )

    pending = []

    def start(condition, item):
        pending.append((condition, item))
        if condition is None:
            item.start()
        else:
            pl.when(condition)(item.start)

    def part(ref, k):
        return ref.at[:, pl.ds(k * chunk, chunk), :]

    barrier = pltpu.get_barrier_semaphore()
    for device in [up, down, mid_to, end_to] + [xy_to(o) for o in range(1, n_xy)]:
        pl.semaphore_signal(barrier, inc=1, device_id=device, device_id_type=MESH)

    @pl.when(swapped)
    def _():
        pl.semaphore_signal(barrier, inc=1, device_id=swap_to, device_id_type=MESH)
        pl.semaphore_wait(barrier, 4 + n_xy)

    @pl.when(jnp.logical_not(swapped))
    def _():
        pl.semaphore_wait(barrier, 3 + n_xy)

    def z_copies(kind, s, k):
        source, halo = (vel, vhalo) if kind == "v" else (sz, shalo)
        return (
            copy((kind, s, 0, k), part(source.at[s], k), part(halo.at[s, 0], k), up),
            copy((kind, s, 1, k), part(source.at[s], k), part(halo.at[s, 1], k), down),
        )

    def z_start(kind, s, k):
        upward, downward = z_copies(kind, s, k)
        pending.extend([(has_up, upward), (has_down, downward)])
        pl.when(jnp.logical_and(has_up, grp == 1))(upward.start)
        pl.when(has_down)(downward.start)
        pl.when(jnp.logical_and(has_up, grp == 0))(upward.start)

    def z_wait(kind, s, k):
        upward, downward = z_copies(kind, s, k)
        pl.when(has_down)(upward.wait_recv)
        pl.when(has_up)(downward.wait_recv)

    swap_in = [copy(("in", k), part(in_ref, k), part(vel.at[0], k), swap_to) for k in range(CHUNKS)]
    for k in range(CHUNKS):
        start(swapped, swap_in[k])

    @pl.when(jnp.logical_not(swapped))
    def _():
        vel[0] = in_ref[...]

    @pl.when(level == 0)
    def _():
        for s in range(STEPS):
            vhalo[s, 0] = jnp.zeros_like(vel[0])
            shalo[s, 0] = jnp.zeros_like(vel[0])

    @pl.when(level == levels - 1)
    def _():
        for s in range(STEPS):
            vhalo[s, 1] = jnp.zeros_like(vel[0])
            shalo[s, 1] = jnp.zeros_like(vel[0])

    for k in range(CHUNKS):
        pl.when(swapped)(swap_in[k].wait_recv)
        z_start("v", 0, k)

    picker = jnp.where(
        lax.broadcasted_iota(jnp.int32, (cols_all, width), 0) == cols_ref[...], 1.0, 0.0
    ).astype(jnp.bfloat16)

    def picked(field):
        high = field.astype(jnp.bfloat16)
        rest = field - high.astype(jnp.float32)
        middle = rest.astype(jnp.bfloat16)
        low = (rest - middle.astype(jnp.float32)).astype(jnp.bfloat16)
        return (dot(high, picker) + (dot(middle, picker) + dot(low, picker))) * weight_ref[...]

    def x_derived(field):
        left, right = field[:, :half], field[:, half:]
        total = dot_parts(halves(left + right), (mx_ref[0], mx_ref[1]))
        difference = dot_parts(halves(left - right), (mx_ref[2], mx_ref[3]))
        return jnp.concatenate([total + difference, total - difference], axis=1)

    def compress(index, read):
        def body(c, carry):
            gsend[index, c] = dot_parts((gather_ref[0], gather_ref[1]), halves(read(c)))
            return carry

        lax.fori_loop(0, 3, body, 0)
        for o in range(1, n_xy):
            start(None, compressed(index, o))

    def compressed(index, o):
        return copy(("g", index, o), gsend.at[index], grecv.at[index, o - 1], xy_to(o))

    def received(index, c):
        result = None
        for o in range(1, n_xy):
            term = dot_parts((spread_ref[0, o - 1], spread_ref[1, o - 1]), halves(grecv[index, o - 1, c]))
            result = term if result is None else result + term
        return result

    def g_wait(index):
        for o in range(1, n_xy):
            compressed(index, o).wait_recv()

    z_scale = 1.0 / (2.0 * level_gap)

    for s in range(STEPS):
        compress(2 * s, lambda c: vel[s, c])

        def first(c, carry):
            field = vel[s, c]
            gx[c] = x_derived(field)
            gy[c] = dot_parts((my_ref[0], my_ref[1]), halves(field))
            return carry

        lax.fori_loop(0, 3, first, 0)
        g_wait(2 * s)

        def second(c, carry):
            gy[c] = gy[c] + received(2 * s, c)
            return carry

        if n_xy > 1:
            lax.fori_loop(0, 3, second, 0)

        def pointwise(i, carry):
            rows = pl.ds(pl.multiple_of(i * ROWS, ROWS), ROWS)
            u = [vel[s, c, rows, :] for c in range(3)]
            dx = [gx[c, rows, :] for c in range(3)]
            dy = [gy[c, rows, :] for c in range(3)]
            dz = [(vhalo[s, 1, c, rows, :] - vhalo[s, 0, c, rows, :]) * z_scale for c in range(3)]
            for c in range(3):
                tend[c, rows, :] = -(u[0] * dx[c] + u[1] * dy[c] + u[2] * dz[c])
            xx, yy, zz = dx[0], dy[1], dz[2]
            xy_, xz, yz = 0.5 * (dy[0] + dx[1]), 0.5 * (dz[0] + dx[2]), 0.5 * (dz[1] + dy[2])
            total = xx * xx + yy * yy + zz * zz + 2.0 * (xy_ * xy_ + xz * xz + yz * yz)
            eddy = (2.0 * scale) * jnp.sqrt(2.0 * total)
            xy_, xz, yz = eddy * xy_, eddy * xz, eddy * yz
            sx[0, rows, :] = eddy * xx
            sx[1, rows, :] = xy_
            sx[2, rows, :] = xz
            sy[0, rows, :] = xy_
            sy[1, rows, :] = eddy * yy
            sy[2, rows, :] = yz
            sz[s, 0, rows, :] = xz
            sz[s, 1, rows, :] = yz
            sz[s, 2, rows, :] = eddy * zz
            return carry

        for k in range(CHUNKS):
            z_wait("v", s, k)
            lax.fori_loop(k * chunk // ROWS, (k + 1) * chunk // ROWS, pointwise, 0)
            z_start("s", s, k)

        compress(2 * s + 1, lambda c: sy[c])

        def third(c, carry):
            local = dot_parts((my_ref[0], my_ref[1]), halves(sy[c]))
            tend[c] = tend[c] + x_derived(sx[c]) + local
            return carry

        lax.fori_loop(0, 3, third, 0)
        g_wait(2 * s + 1)

        def fourth(c, carry):
            tend[c] = tend[c] + received(2 * s + 1, c)
            return carry

        if n_xy > 1:
            lax.fori_loop(0, 3, fourth, 0)

        last = s == STEPS - 1

        def updated(k, target):
            def body(i, carry):
                rows = pl.ds(pl.multiple_of(i * ROWS, ROWS), ROWS)
                for c in range(3):
                    along_z = (shalo[s, 1, c, rows, :] - shalo[s, 0, c, rows, :]) * z_scale
                    target[c, rows, :] = vel[s, c, rows, :] + time_step * (tend[c, rows, :] + along_z)
                return carry

            lax.fori_loop(k * chunk // ROWS, (k + 1) * chunk // ROWS, body, 0)

        def pick(k, source):
            rows = pl.ds(k * chunk, chunk)
            for c in range(3):
                psend[s, c, rows, :] = picked(source[c, rows, :])

        def blend(k, source, target):
            rows = pl.ds(k * chunk, chunk)
            for c in range(3):
                own = source[c, rows, :width] * (1.0 - weight_ref[...])
                target[c, rows, :width] = own + precv[s, c, rows, :]

        def fringe_copy(k, device):
            return copy(("f", s, k), part(psend.at[s], k), part(precv.at[s], k), device)

        if not last:
            following = vel.at[s + 1]
            for k in range(CHUNKS):
                z_wait("s", s, k)
                updated(k, following)

                @pl.when(jnp.logical_not(is_farm))
                def _():
                    pick(k, following)

                start(jnp.logical_not(is_farm), fringe_copy(k, mid_to))

                @pl.when(is_farm)
                def _():
                    fringe_copy(k, mid_to).wait_recv()
                    blend(k, following, following)

                z_start("v", s + 1, k)
        else:
            back = [copy(("out", k), part(ret, k), part(fin, k), swap_to) for k in range(CHUNKS)]
            for k in range(CHUNKS):
                z_wait("s", s, k)

                @pl.when(swapped)
                def _():
                    updated(k, ret)

                @pl.when(jnp.logical_not(swapped))
                def _():
                    updated(k, fin)

                start(swapped, back[k])
            for k in range(CHUNKS):
                pl.when(swapped)(back[k].wait_recv)

                @pl.when(grp == 1)
                def _():
                    pick(k, fin)

                start(grp == 1, fringe_copy(k, end_to))
                rows = pl.ds(k * chunk, chunk)
                out_ref[:, rows, :] = fin[:, rows, :]

                @pl.when(grp == 0)
                def _():
                    fringe_copy(k, end_to).wait_recv()
                    blend(k, fin, out_ref)

    for condition, item in pending:
        if condition is None:
            item.wait_send()
        else:
            pl.when(condition)(item.wait_send)


def per_device(velocity, fringe_columns):
    _, comps, _, rows_all, cols_all = velocity.shape
    n_xy, n_gz = lax.axis_size("xy"), lax.axis_size("gz")
    cross = rows_all * n_xy
    delta = (2.0 * math.pi / cols_all * (2.0 * math.pi / cross) * level_gap) ** (1.0 / 3.0)
    width = fringe_columns.shape[0]
    half = cols_all // 2
    along = derivative_matrix(cols_all).T
    same, other = along[:half, :half], along[half:, :half]
    mx = np.concatenate([two_parts((same + other) / 2), two_parts((same - other) / 2)])
    across = derivative_matrix(cross)
    my = two_parts(across[:rows_all, :rows_all])
    if n_xy > 1:
        spread, gather = factored(across[rows_all:, :rows_all])
    else:
        spread, gather = np.zeros((rows_all, 16)), np.zeros((16, rows_all))
    rank = gather.shape[0]
    gather = two_parts(gather)
    spread = two_parts(spread).reshape(2, -1, rows_all, rank)
    others = spread.shape[1]
    offsets = np.arange(width)
    weights = (0.5 * (1.0 + np.cos(np.pi * offsets / width))).astype(np.float32)[None]
    plane = (comps, rows_all, cols_all)
    fringe = (comps, rows_all, width)
    copies = STEPS * CHUNKS * 5 + 2 * CHUNKS + 2 * STEPS * others
    vmem = pl.BlockSpec(memory_space=pltpu.VMEM)

    def buffer(*shape):
        return pltpu.VMEM(shape, jnp.float32)

    result = pl.pallas_call(
        functools.partial(kernel, (n_gz, n_xy, width, (smag_coeff * delta) ** 2)),
        out_shape=jax.ShapeDtypeStruct(plane, jnp.float32),
        in_specs=[vmem] * 7,
        out_specs=vmem,
        scratch_shapes=[
            buffer(STEPS, *plane),
            buffer(*plane),
            buffer(*plane),
            buffer(STEPS, 2, *plane),
            buffer(STEPS, 2, *plane),
            buffer(*plane),
            buffer(*plane),
            buffer(*plane),
            buffer(*plane),
            buffer(*plane),
            buffer(STEPS, *plane),
            buffer(2 * STEPS, comps, rank, cols_all),
            buffer(2 * STEPS, others, comps, rank, cols_all),
            buffer(STEPS, *fringe),
            buffer(STEPS, *fringe),
            pltpu.SemaphoreType.DMA((copies,)),
            pltpu.SemaphoreType.DMA((copies,)),
        ],
        compiler_params=pltpu.CompilerParams(
            collective_id=0, has_side_effects=True, vmem_limit_bytes=56 * 1024 * 1024
        ),
    )(
        velocity.reshape(plane), fringe_columns.reshape(1, width), jnp.asarray(weights),
        jnp.asarray(mx), jnp.asarray(my), jnp.asarray(gather), jnp.asarray(spread),
    )
    return result.reshape(velocity.shape)


def solution(mesh):
    in_specs = (P("grp", None, "gz", "xy", None), P())
    out_specs = P("grp", None, "gz", "xy", None)
    return jax.shard_map(
        per_device, mesh=mesh, in_specs=in_specs, out_specs=out_specs, check_vma=False
    )
```
